512 devices in a mesh: row: 16 (over z_hi, y), col: 32 (over x, z_lo, core).
Axes of the slice: x: 4, y: 8, z: 8 (z_hi: 2, z_lo: 4; z = z_hi * 4 + z_lo), core: 2. Of those that a mesh axis runs over, the one named last changes fastest.
Arguments:
- query_act: bfloat16 [768, 16384], P(None, 'row'), may hold values from -6 to 6
- query_grad: bfloat16 [768, 16384], P(None, 'col'), may hold values from -6 to 6
- train_rot: bfloat16 [384, 16384], P(None, 'col'), may hold values from -6 to 6
- basis_in: bfloat16 [16384, 16384], P('row', 'col'), may hold values from -0.046875 to 0.046875
- basis_out: bfloat16 [16384, 16384], P('col', 'row'), may hold values from -0.046875 to 0.046875
- eig_in: float32 [16384], replicated, may hold values from 0.05 to 2
- eig_out: float32 [16384], replicated, may hold values from 0.05 to 2
Outputs:
- predicted: float32 [384, 16384], P('row', 'col')
The draws below stay inside these ranges and needn't reach their ends.
All inputs are finite; a program needn't handle non-finite values.
Results may differ from the reference program's by a relative error of at most 0.0049.
Values may be sent and summed in bfloat16 or wider, within the bound.
No kernel may reach another device: no remote copies, remote signals or barrier semaphores. Data moves between devices by JAX's collectives and lax.ppermute only.
A program may use at most 64 MiB of HBM per device.

```python
import math
import jax
import jax.numpy as jnp
from jax import lax

DI = 16384
DO = 16384
QUERIES = 768
TRAIN = 384


def steps_of(key, extent, split, low, high):
    level = 1.0
    for dim, parts in split:
        steps = jax.random.uniform(jax.random.fold_in(jax.random.fold_in(key, 6), dim), (parts,), jnp.float32, low / len(split), high / len(split))
        level = level * jnp.repeat(jnp.exp(steps), extent[dim] // parts).reshape((-1,) + (1,) * (len(extent) - 1 - dim))
    return level


def scatter_about(own_key, dims, width, reach, shards=(), kind=jnp.bfloat16):
    result = jax.random.normal(own_key, dims, jnp.float32) * width
    if len(shards) > 0:
        result = steps_of(own_key, dims, shards, -0.22, 0.18) * result
    return jnp.clip(result, min=-reach, max=reach).astype(kind)


def setup_inputs(seed: int = 0) -> dict:
    keys = jax.random.split(jax.random.key(seed), 8)
    return {
        "query_act": scatter_about(keys[0], (QUERIES, DI), 1.0, 6.0, ((1, 16),)),
        "query_grad": scatter_about(keys[1], (QUERIES, DO), 1.0, 6.0, ((1, 32),)),
        "train_rot": scatter_about(keys[2], (TRAIN, DI), 1.0, 6.0, ((1, 32),)),
        "basis_in": scatter_about(keys[3], (DI, DI), DI ** -0.5, 0.046875, ((0, 16), (1, 32))),
        "basis_out": scatter_about(keys[4], (DO, DO), DO ** -0.5, 0.046875, ((0, 32), (1, 16))),
        "eig_in": jnp.clip(jnp.exp(jax.random.uniform(keys[5], (DI,), jnp.float32, math.log(0.05), math.log(2.0))), 0.05, 2.0),
        "eig_out": jnp.clip(jnp.exp(jax.random.uniform(keys[6], (DO,), jnp.float32, math.log(0.05), math.log(2.0))), 0.05, 2.0),
    }


damping_share = 0.1

def math_sqrt(value):
    return float(value) ** 0.5

def reference(query_act, query_grad, train_rot, basis_in, basis_out, eig_in, eig_out):
    act_rot = jnp.dot(query_act, basis_in, preferred_element_type=jnp.float32).astype(jnp.bfloat16)
    grad_rot = jnp.dot(query_grad, basis_out, preferred_element_type=jnp.float32).astype(jnp.bfloat16)
    damp = damping_share * jnp.mean(eig_in) * jnp.mean(eig_out)
    block = min(DO, 1024)
    count = DO // block

    def one_block(index):
        start = (index * block).astype(jnp.int32)
        grad_part = lax.dynamic_slice_in_dim(grad_rot, start, block, 1)
        eig_part = lax.dynamic_slice_in_dim(eig_out, start, block, 0)
        outer = lax.dot_general(grad_part, act_rot, (((0,), (0,)), ((), ())), preferred_element_type=jnp.float32)
        scaled = (outer / QUERIES / (eig_part[:, None] * eig_in[None, :] + damp)).astype(jnp.bfloat16)
        return lax.dot_general(train_rot, scaled, (((1,), (1,)), ((), ())), preferred_element_type=jnp.float32)
    pieces = lax.map(one_block, jnp.arange(count, dtype=jnp.int32))
    inner = jnp.transpose(pieces, (1, 0, 2)).reshape(TRAIN, DO)
    inner = (inner * (1.0 / math_sqrt(DI))).astype(jnp.bfloat16)
    return lax.dot_general(inner, basis_out, (((1,), (1,)), ((), ())), preferred_element_type=jnp.float32)
```

```python
import functools

import jax
import jax.numpy as jnp
import numpy as np
from jax import lax
from jax.experimental import pallas as pl
from jax.experimental.pallas import tpu as pltpu
from jax.sharding import Mesh
from jax.sharding import PartitionSpec as P

ROW = ("z_hi", "y")
CHIPS = ("x", "z_lo")
COL = ("x", "z_lo", "core")
ALL = ROW + COL
SIZES = (2, 8, 4, 4, 2)
SWAP = [(0, 1), (1, 0)]

damping_share = 0.1

bf16 = jnp.bfloat16
f32 = jnp.float32


def mixed_groups():
    ids = np.arange(np.prod(SIZES)).reshape(16, 16, 2)
    along_row = [ids[:, c, 0].tolist() for c in range(16)]
    along_col = [ids[r, :, 1].tolist() for r in range(16)]
    return along_row + along_col


def dot(a, b):
    return jnp.dot(a, b, preferred_element_type=f32)


def dot_nt(a, b):
    return lax.dot_general(a, b, (((1,), (1,)), ((), ())), preferred_element_type=f32)


def dot_tn(a, b):
    return lax.dot_general(a, b, (((0,), (0,)), ((), ())), preferred_element_type=f32)


def rotate_kernel(core, act, grad, b_in, b_out, b_in_o, grad_o, b_out_o, out):
    tile = 256
    half = b_in.shape[1]

    @pl.when(core[0] == 0)
    def _():
        @pl.loop(0, act.shape[0] // tile)
        def _(m):
            rows = pl.ds(pl.multiple_of(m * tile, tile), tile)
            left = act[rows, :]
            out[rows, :half] = dot(left, b_in[...]).astype(bf16)
            out[rows, half:] = dot(left, b_in_o[...]).astype(bf16)

    @pl.when(core[0] == 1)
    def _():
        @pl.loop(0, act.shape[0] // tile)
        def _(m):
            rows = pl.ds(pl.multiple_of(m * tile, tile), tile)
            out[rows, :] = (
                dot(grad_o[rows, :], b_out_o[...]) + dot(grad[rows, :], b_out[...])
            ).astype(bf16)


def outer_kernel(queries, core, damp, own, other, train, train_o, e_out, e_in, out):
    tile = 256
    half = train.shape[1]

    def body(act, grad, first, left, right):
        @pl.loop(0, half // tile)
        def _(m):
            start = pl.multiple_of(m * tile, tile)
            outer = dot_tn(grad[:, pl.ds(first + start, tile)], act[...])
            scaled = (
                outer / queries / (e_out[pl.ds(start, tile), :] * e_in[...] + damp[0])
            ).astype(bf16)
            out[:, pl.ds(start, tile)] = (
                dot_nt(left[...], scaled[:, :half]) + dot_nt(right[...], scaled[:, half:])
            ).astype(bf16)

    @pl.when(core[0] == 0)
    def _():
        body(own, other, 0, train, train_o)

    @pl.when(core[0] == 1)
    def _():
        body(other, own, half, train_o, train)


def back_kernel(core, own, other, b_out, out):
    half = own.shape[1]

    def body(left, right):
        out[...] = (
            dot_nt(left[...], b_out[:, :half]) + dot_nt(right[...], b_out[:, half:])
        ).astype(bf16)

    @pl.when(core[0] == 0)
    def _():
        body(own, other)

    @pl.when(core[0] == 1)
    def _():
        body(other, own)


def call(kernel, shape, scalars, arrays, flops):
    return pl.pallas_call(
        kernel,
        out_shape=jax.ShapeDtypeStruct(shape, bf16),
        in_specs=[pl.BlockSpec(memory_space=pltpu.SMEM)] * len(scalars)
        + [pl.BlockSpec(memory_space=pltpu.VMEM)] * len(arrays),
        out_specs=pl.BlockSpec(memory_space=pltpu.VMEM),
        compiler_params=pltpu.CompilerParams(vmem_limit_bytes=32 * 1024 * 1024),
        cost_estimate=pl.CostEstimate(flops=flops, bytes_accessed=4 << 20, transcendentals=0),
    )(*scalars, *arrays)


def summed(pieces):
    return jnp.sum(pieces.astype(f32), axis=0)


def spread(array, n):
    return jnp.broadcast_to(array[None], (n, *array.shape))


def per_device(query_act, query_grad, train_rot, basis_in, basis_out, eig_in, eig_out):
    queries, train = query_act.shape[0], train_rot.shape[0]
    width = basis_in.shape[0]
    half = basis_in.shape[1]
    groups = mixed_groups()
    mixed = functools.partial(
        lax.all_to_all,
        axis_name=ALL,
        split_axis=0,
        concat_axis=0,
        axis_index_groups=groups,
        tiled=True,
    )
    core_id = lax.axis_index("core")
    core = core_id.astype(jnp.int32).reshape(1)

    basis_in_o = lax.ppermute(basis_in, "core", [(1, 0)])
    basis_out_o = lax.ppermute(basis_out, "core", [(0, 1)])
    grad_o = lax.ppermute(query_grad, "core", [(0, 1)])
    train_o = lax.ppermute(train_rot, "core", SWAP)

    part = call(
        rotate_kernel,
        (queries, width),
        (core,),
        (query_act, query_grad, basis_in, basis_out, basis_in_o, grad_o, basis_out_o),
        2 * queries * width * width,
    )
    rot = summed(mixed(part.reshape(16, queries // 16, width))).astype(bf16)
    own = mixed(spread(rot, 16)).reshape(queries, width)
    other = lax.ppermute(own, "core", SWAP)

    damp = damping_share * jnp.mean(eig_in) * jnp.mean(eig_out)
    out_start = lax.axis_index(ROW) * width + core_id * half
    in_start = lax.axis_index(CHIPS) * width
    e_out = lax.dynamic_slice_in_dim(eig_out, out_start, half, 0)[:, None]
    e_in = lax.dynamic_slice_in_dim(eig_in, in_start, width, 0)[None, :]
    partial_inner = call(
        functools.partial(outer_kernel, queries),
        (train, half),
        (core, damp.reshape(1)),
        (own, other, train_rot, train_o, e_out, e_in),
        2 * queries * width * half + 2 * train * width * half,
    )
    pieces = lax.all_to_all(
        partial_inner.reshape(16, train // 16, half), CHIPS, 0, 0, tiled=True
    )
    factor = 1.0 / float(eig_in.shape[0]) ** 0.5
    inner_part = (summed(pieces) * factor).astype(bf16)
    inner = lax.all_to_all(spread(inner_part, 16), CHIPS, 0, 0, tiled=True).reshape(train, half)
    inner_o = lax.ppermute(inner, "core", SWAP)
    partial_out = call(
        back_kernel,
        (train, half),
        (core,),
        (inner, inner_o, basis_out),
        2 * train * half * width,
    )
    return summed(
        lax.all_to_all(partial_out.reshape(16, train // 16, half), ROW, 0, 0, tiled=True)
    )


def solution(mesh):
    split = Mesh(mesh.devices.reshape(SIZES), ALL)
    placed = (P(None, ROW), P(None, COL), P(None, COL), P(ROW, COL), P(COL, ROW), P(), P())
    return jax.shard_map(
        per_device, mesh=split, in_specs=placed, out_specs=P(ROW, COL), check_vma=False
    )
```

```python
import functools

import jax
import jax.numpy as jnp
import numpy as np
from jax import lax
from jax.experimental import pallas as pl
from jax.experimental.pallas import tpu as pltpu
from jax.sharding import Mesh
from jax.sharding import PartitionSpec as P

ROW = ("z_hi", "y")
CHIPS = ("x", "z_lo")
COL = ("x", "z_lo", "core")
ALL = ROW + COL
SIZES = (2, 8, 4, 4, 2)
SWAP = [(0, 1), (1, 0)]

damping_share = 0.1

bf16 = jnp.bfloat16
f32 = jnp.float32


def mixed_groups():
    ids = np.arange(np.prod(SIZES)).reshape(2, 8, 4, 2, 2, 2)
    along_row = ids[..., 0].transpose(0, 2, 3, 4, 1).reshape(-1, 8).tolist()
    along_col = ids[..., 1].transpose(0, 1, 3, 2, 4).reshape(-1, 8).tolist()
    return along_row + along_col


def mixed_pairs():
    ids = np.arange(np.prod(SIZES)).reshape(2, 8, 4, 2, 2, 2)
    to = np.empty_like(ids)
    to[..., 0] = ids[::-1, ..., 0]
    to[..., 1] = ids[:, :, :, ::-1, :, 1]
    return list(zip(ids.reshape(-1).tolist(), to.reshape(-1).tolist()))


def dot(a, b):
    return jnp.dot(a, b, preferred_element_type=f32)


def dot_nt(a, b):
    return lax.dot_general(a, b, (((1,), (1,)), ((), ())), preferred_element_type=f32)


def dot_tn(a, b):
    return lax.dot_general(a, b, (((0,), (0,)), ((), ())), preferred_element_type=f32)


TILE = 256


def rotate_kernel(core, b_in_o, grad_o, b_out_o, act, grad, b_in, b_out, out, left, in_w, out_w, sems):
    half = grad_o.shape[1]
    steps = left.shape[0] // TILE

    def bring(source, held, weight, room):
        load = pltpu.make_async_copy(weight, room, sems.at[steps])
        rows = [
            pltpu.make_async_copy(
                source.at[pl.ds(m * TILE, TILE)], held.at[pl.ds(m * TILE, TILE)], sems.at[m]
            )
            for m in range(steps)
        ]
        rows[0].start()
        load.start()
        for copy in rows[1:]:
            copy.start()
        rows[0].wait()
        load.wait()
        for m, copy in enumerate(rows):
            if m:
                copy.wait()
            yield pl.ds(m * TILE, TILE)

    @pl.when(core[0] == 0)
    def _():
        for rows in bring(act, left, b_in, in_w):
            out[rows, :half] = dot(left[rows, :], in_w[...]).astype(bf16)
            out[rows, half:] = dot(left[rows, :], b_in_o[...]).astype(bf16)

    @pl.when(core[0] == 1)
    def _():
        held = left.at[:, :half]
        for rows in bring(grad, held, b_out, out_w):
            out[rows, :] = (
                dot(grad_o[rows, :], b_out_o[...]) + dot(held[rows, :], out_w[...])
            ).astype(bf16)


def outer_kernel(queries, core, damp, own, other, train, train_o, e_out, e_in, out):
    tile = 256
    half = train.shape[1]

    def body(act, grad, first, left, right):
        @pl.loop(0, half // tile)
        def _(m):
            start = pl.multiple_of(m * tile, tile)
            outer = dot_tn(grad[:, pl.ds(first + start, tile)], act[...])
            scaled = (
                outer / queries / (e_out[pl.ds(start, tile), :] * e_in[...] + damp[0])
            ).astype(bf16)
            out[:, pl.ds(start, tile)] = (
                dot_nt(left[...], scaled[:, :half]) + dot_nt(right[...], scaled[:, half:])
            ).astype(bf16)

    @pl.when(core[0] == 0)
    def _():
        body(own, other, 0, train, train_o)

    @pl.when(core[0] == 1)
    def _():
        body(other, own, half, train_o, train)


def back_kernel(core, own, other, b_out, out):
    half = own.shape[1]

    def body(left, right):
        out[...] = (
            dot_nt(left[...], b_out[:, :half]) + dot_nt(right[...], b_out[:, half:])
        ).astype(bf16)

    @pl.when(core[0] == 0)
    def _():
        body(own, other)

    @pl.when(core[0] == 1)
    def _():
        body(other, own)


def call(kernel, shape, scalars, arrays, flops, far=0, scratch=()):
    anywhere = pl.BlockSpec(memory_space=pl.ANY)
    in_vmem = pl.BlockSpec(memory_space=pltpu.VMEM)
    return pl.pallas_call(
        kernel,
        out_shape=jax.ShapeDtypeStruct(shape, bf16),
        in_specs=[pl.BlockSpec(memory_space=pltpu.SMEM)] * len(scalars)
        + [in_vmem] * (len(arrays) - far)
        + [anywhere] * far,
        out_specs=in_vmem,
        scratch_shapes=scratch,
        compiler_params=pltpu.CompilerParams(vmem_limit_bytes=(51 if far else 32) * 1024 * 1024),
        cost_estimate=pl.CostEstimate(flops=flops, bytes_accessed=4 << 20, transcendentals=0),
    )(*scalars, *arrays)


def summed(pieces):
    return jnp.sum(pieces.astype(f32), axis=0)


def spread(array, n):
    return jnp.broadcast_to(array[None], (n, *array.shape))


def per_device(query_act, query_grad, train_rot, basis_in, basis_out, eig_in, eig_out):
    queries, train = query_act.shape[0], train_rot.shape[0]
    width = basis_in.shape[0]
    half = basis_in.shape[1]
    groups = mixed_groups()
    mixed = functools.partial(
        lax.all_to_all,
        axis_name=ALL,
        split_axis=0,
        concat_axis=0,
        axis_index_groups=groups,
        tiled=True,
    )
    core_id = lax.axis_index("core")
    core = core_id.astype(jnp.int32).reshape(1)

    basis_in_o = lax.ppermute(basis_in, "core", [(1, 0)])
    basis_out_o = lax.ppermute(basis_out, "core", [(0, 1)])
    grad_o = lax.ppermute(query_grad, "core", [(0, 1)])

    part = call(
        rotate_kernel,
        (queries, width),
        (core,),
        (basis_in_o, grad_o, basis_out_o, query_act, query_grad, basis_in, basis_out),
        2 * queries * width * width,
        far=4,
        scratch=(
            pltpu.VMEM((queries, width), bf16),
            pltpu.VMEM((width, half), bf16),
            pltpu.VMEM((half, width), bf16),
            pltpu.SemaphoreType.DMA((queries // TILE + 1,)),
        ),
    )
    damp = damping_share * jnp.mean(eig_in) * jnp.mean(eig_out)
    out_start = lax.axis_index(ROW) * width + core_id * half
    in_start = lax.axis_index(CHIPS) * width
    e_out = lax.dynamic_slice_in_dim(eig_out, out_start, half, 0)[:, None]
    e_in = lax.dynamic_slice_in_dim(eig_in, in_start, width, 0)[None, :]
    part, damp, e_out, e_in = lax.optimization_barrier((part, damp, e_out, e_in))

    eighth = summed(mixed(part.reshape(8, queries // 8, width)))
    eighth, train_rot = lax.optimization_barrier((eighth, train_rot))
    far_sum = lax.ppermute(eighth.astype(bf16), ALL, mixed_pairs())
    train_o = lax.ppermute(train_rot, "core", SWAP)
    rot = (eighth + far_sum.astype(f32)).astype(bf16)
    rot, train_o = lax.optimization_barrier((rot, train_o))
    own = mixed(spread(rot, 8)).reshape(queries, width)
    other = lax.ppermute(own, "core", SWAP)

    partial_inner = call(
        functools.partial(outer_kernel, queries),
        (train, half),
        (core, damp.reshape(1)),
        (own, other, train_rot, train_o, e_out, e_in),
        2 * queries * width * half + 2 * train * width * half,
    )
    pieces = lax.all_to_all(
        partial_inner.reshape(16, train // 16, half), CHIPS, 0, 0, tiled=True
    )
    factor = 1.0 / float(eig_in.shape[0]) ** 0.5
    inner_part = (summed(pieces) * factor).astype(bf16)
    inner = lax.all_to_all(spread(inner_part, 16), CHIPS, 0, 0, tiled=True).reshape(train, half)
    inner_o = lax.ppermute(inner, "core", SWAP)
    partial_out = call(
        back_kernel,
        (train, half),
        (core,),
        (inner, inner_o, basis_out),
        2 * train * half * width,
    )
    return summed(
        lax.all_to_all(partial_out.reshape(16, train // 16, half), ROW, 0, 0, tiled=True)
    )


def solution(mesh):
    split = Mesh(mesh.devices.reshape(SIZES), ALL)
    placed = (P(None, ROW), P(None, COL), P(None, COL), P(ROW, COL), P(COL, ROW), P(), P())
    return jax.shard_map(
        per_device, mesh=split, in_specs=placed, out_specs=P(ROW, COL), check_vma=False
    )
```

```python
import functools

import jax
import jax.numpy as jnp
import numpy as np
from jax import lax
from jax.experimental import pallas as pl
from jax.experimental.pallas import tpu as pltpu
from jax.sharding import Mesh
from jax.sharding import PartitionSpec as P

ROW = ("z_hi", "y")
CHIPS = ("x", "z_a", "z_b")
COL = (*CHIPS, "core")
ALL = ROW + COL
SIZES = (2, 8, 4, 2, 2, 2)
NEAR = ("x", "z_b")
SWAP = [(0, 1), (1, 0)]
MIB = 1024 * 1024

damping_share = 0.1

bf16 = jnp.bfloat16
f32 = jnp.float32

SMEM = pl.BlockSpec(memory_space=pltpu.SMEM)
VMEM = pl.BlockSpec(memory_space=pltpu.VMEM)
ANY = pl.BlockSpec(memory_space=pl.ANY)


def mixed_groups():
    ids = np.arange(np.prod(SIZES)).reshape(SIZES)
    along_row = ids[..., 0].transpose(0, 2, 3, 4, 1).reshape(-1, 8).tolist()
    along_col = ids[..., 1].transpose(0, 1, 3, 2, 4).reshape(-1, 8).tolist()
    return along_row + along_col


def mixed_pairs():
    ids = np.arange(np.prod(SIZES)).reshape(SIZES)
    to = np.empty_like(ids)
    to[..., 0] = ids[::-1, ..., 0]
    to[..., 1] = ids[:, :, :, ::-1, :, 1]
    return list(zip(ids.reshape(-1).tolist(), to.reshape(-1).tolist()))


def dot(a, b):
    return jnp.dot(a, b, preferred_element_type=f32)


def dot_nt(a, b):
    return lax.dot_general(a, b, (((1,), (1,)), ((), ())), preferred_element_type=f32)


def dot_tn(a, b):
    return lax.dot_general(a, b, (((0,), (0,)), ((), ())), preferred_element_type=f32)


TILE = 256


def damp_kernel(e_in, e_out, damp):
    damp[0] = (
        damping_share * (jnp.sum(e_in[...]) / e_in.size) * (jnp.sum(e_out[...]) / e_out.size)
    )


def rotate_kernel(place, act, grad, b_in, b_out, b_in_o, grad_o, b_out_o, first, second):
    half = grad.shape[1]
    tile = 128
    steps = first.shape[0] // tile

    def body(product):
        for index, out in enumerate((first, second)):

            @pl.loop(0, steps)
            def _(m):
                to = pl.ds(pl.multiple_of(m * tile, tile), tile)
                product(out, to, pl.ds(pl.multiple_of((index * steps + m) * tile, tile), tile))

    def joined(out, to, rows):
        out[to, :half] = dot(act[rows, :], b_in[...]).astype(bf16)
        out[to, half:] = dot(act[rows, :], b_in_o[...]).astype(bf16)

    def added(out, to, rows):
        out[to, :] = (dot(grad_o[rows, :], b_out_o[...]) + dot(grad[rows, :], b_out[...])).astype(bf16)

    @pl.when(place[0] == 0)
    def _():
        body(joined)

    @pl.when(place[0] == 1)
    def _():
        body(added)


def outer_kernel(queries, place, damp, own_a, own_b, other_a, other_b, train, train_o, e_out, e_in, out):
    half = train.shape[1]
    lanes = e_in.shape[1]
    units = 8 * lanes
    e_rows = e_in[pl.ds(pl.multiple_of(place[1] * 8, 8), 8), :]
    e_row = jnp.concatenate([e_rows[r : r + 1, :] for r in range(units // lanes)], axis=1)
    e_cols = jnp.transpose(e_out[pl.ds(pl.multiple_of(place[2] * 8, 8), 8), :])

    def body(acts, grads, first, left, right):
        for start in range(0, half, TILE):
            outer = sum(
                dot_tn(grad[:, first + start : first + start + TILE], act[...])
                for act, grad in zip(acts, grads)
            )
            r = (first + start) // lanes
            e_col = jnp.concatenate([e_cols[:, r + q : r + q + 1] for q in range(TILE // lanes)], axis=0)
            scaled = (outer / queries / (e_col * e_row + damp[0])).astype(bf16)
            out[:, start : start + TILE] = (
                dot_nt(left[...], scaled[:, :half]) + dot_nt(right[...], scaled[:, half:])
            ).astype(bf16)

    @pl.when(place[0] == 0)
    def _():
        body((own_a, own_b), (other_a, other_b), 0, train, train_o)

    @pl.when(place[0] == 1)
    def _():
        body((other_a, other_b), (own_a, own_b), half, train_o, train)


def back_kernel(place, own, other, b_out, out):
    half = own.shape[1]

    def body(left, right):
        out[...] = (
            dot_nt(left[...], b_out[:, :half]) + dot_nt(right[...], b_out[:, half:])
        ).astype(bf16)

    @pl.when(place[0] == 0)
    def _():
        body(own, other)

    @pl.when(place[0] == 1)
    def _():
        body(other, own)


def call(kernel, args, specs, shapes, out_specs, flops, limit, scratch=()):
    return pl.pallas_call(
        kernel,
        out_shape=shapes,
        in_specs=specs,
        out_specs=out_specs,
        scratch_shapes=scratch,
        compiler_params=pltpu.CompilerParams(vmem_limit_bytes=limit * MIB),
        cost_estimate=pl.CostEstimate(flops=flops, bytes_accessed=4 * MIB, transcendentals=0),
    )(*args)


def summed(pieces):
    return jnp.sum(pieces.astype(f32), axis=0)


def spread(array, n):
    return jnp.broadcast_to(array[None], (n, *array.shape))


def per_device(query_act, query_grad, train_rot, basis_in, basis_out, eig_in, eig_out):
    queries, train = query_act.shape[0], train_rot.shape[0]
    width, half = basis_in.shape
    mixed = functools.partial(
        lax.all_to_all,
        axis_name=ALL,
        split_axis=0,
        concat_axis=0,
        axis_index_groups=mixed_groups(),
        tiled=True,
    )
    near = functools.partial(
        lax.all_to_all, axis_name=NEAR, split_axis=0, concat_axis=0, tiled=True
    )
    shape = jax.ShapeDtypeStruct
    place = jnp.stack(
        [lax.axis_index("core"), lax.axis_index(CHIPS), lax.axis_index(ROW)]
    ).astype(jnp.int32)
    e_in, e_out = (e.reshape(-1, 128) for e in (eig_in, eig_out))

    basis_in_o = lax.ppermute(basis_in, "core", [(1, 0)])
    basis_out_o = lax.ppermute(basis_out, "core", [(0, 1)])
    grad_o = lax.ppermute(query_grad, "core", [(0, 1)])

    damp = call(
        damp_kernel,
        (e_in, e_out),
        [VMEM] * 2,
        shape((1,), f32),
        SMEM,
        6 * 10**9,
        8,
    )
    basis_in_o, basis_out_o, grad_o, damp = lax.optimization_barrier(
        (basis_in_o, basis_out_o, grad_o, damp)
    )
    first, second = call(
        rotate_kernel,
        (place, query_act, query_grad, basis_in, basis_out, basis_in_o, grad_o, basis_out_o),
        [SMEM] + [VMEM] * 7,
        [shape((queries // 2, width), bf16)] * 2,
        [VMEM] * 2,
        2 * queries * width * width,
        32,
    )

    def scatter(part):
        return summed(mixed(part.reshape(8, -1, width)))

    def swap(sums):
        return lax.ppermute(sums.astype(bf16), ALL, mixed_pairs()).astype(f32)

    sum_a = scatter(first)
    sum_a, second, train_rot = lax.optimization_barrier((sum_a, second, train_rot))
    far_a = swap(sum_a)
    train_o = lax.ppermute(train_rot, "core", SWAP)
    sum_b = scatter(second)
    far_a, sum_b, train_o = lax.optimization_barrier((far_a, sum_b, train_o))
    far_b = swap(sum_b)
    own_a = mixed(spread((sum_a + far_a).astype(bf16), 8)).reshape(queries // 2, width)
    far_b, own_a = lax.optimization_barrier((far_b, own_a))
    other_a = lax.ppermute(own_a, "core", SWAP)
    own_b = mixed(spread((sum_b + far_b).astype(bf16), 8)).reshape(queries // 2, width)
    other_b = lax.ppermute(own_b, "core", SWAP)

    partial_inner = call(
        functools.partial(outer_kernel, queries),
        (place, damp, own_a, own_b, other_a, other_b, train_rot, train_o, e_out, e_in),
        [SMEM] * 2 + [VMEM] * 8,
        shape((train, half), bf16),
        VMEM,
        2 * queries * width * half + 2 * train * width * half,
        32,
    )
    inner_sum = summed(near(partial_inner.reshape(8, -1, half)))
    inner_sum = inner_sum + lax.ppermute(inner_sum, "z_a", SWAP)
    factor = 1.0 / float(eig_in.shape[0]) ** 0.5
    inner = near(spread((inner_sum * factor).astype(bf16), 8)).reshape(train, half)
    inner_o = lax.ppermute(inner, "core", SWAP)
    partial_out = call(
        back_kernel,
        (place, inner, inner_o, basis_out),
        [SMEM] + [VMEM] * 3,
        shape((train, half), bf16),
        VMEM,
        2 * train * half * width,
        32,
    )
    return summed(lax.all_to_all(partial_out.reshape(16, -1, half), ROW, 0, 0, tiled=True))


def solution(mesh):
    split = Mesh(mesh.devices.reshape(SIZES), ALL)
    placed = (P(None, ROW), P(None, COL), P(None, COL), P(ROW, COL), P(COL, ROW), P(), P())
    return jax.shard_map(
        per_device, mesh=split, in_specs=placed, out_specs=P(ROW, COL), check_vma=False
    )
```

```python
import functools

import jax
import jax.numpy as jnp
from jax import lax
from jax.experimental import pallas as pl
from jax.experimental.pallas import tpu as pltpu
from jax.sharding import Mesh
from jax.sharding import PartitionSpec as P

ROW = ("z_hi", "y")
CHIPS = ("x", "z_a", "z_b")
COL = (*CHIPS, "core")
ALL = ROW + COL
SIZES = (2, 8, 4, 2, 2, 2)
NEAR = ("x", "z_b")
SWAP = [(0, 1), (1, 0)]
MIB = 1024 * 1024

damping_share = 0.1

bf16 = jnp.bfloat16
f32 = jnp.float32

SMEM = pl.BlockSpec(memory_space=pltpu.SMEM)
VMEM = pl.BlockSpec(memory_space=pltpu.VMEM)
ANY = pl.BlockSpec(memory_space=pl.ANY)


def dot(a, b):
    return jnp.dot(a, b, preferred_element_type=f32)


def dot_nt(a, b):
    return lax.dot_general(a, b, (((1,), (1,)), ((), ())), preferred_element_type=f32)


def dot_tn(a, b):
    return lax.dot_general(a, b, (((0,), (0,)), ((), ())), preferred_element_type=f32)


TILE = 256


def act_kernel(act, weight, out, held, room, sems):
    steps = act.shape[0] // TILE
    pieces = sems.shape[0] - steps
    depth = weight.shape[0] // pieces
    loads = [
        pltpu.make_async_copy(
            weight.at[pl.ds(p * depth, depth)], room.at[pl.ds(p * depth, depth)], sems.at[steps + p]
        )
        for p in range(pieces)
    ]
    spans = [pl.ds(m * TILE, TILE) for m in range(steps)]
    rows = [
        pltpu.make_async_copy(act.at[span], held.at[span], sems.at[m])
        for m, span in enumerate(spans)
    ]
    for copy in loads + rows:
        copy.start()
    for copy in loads:
        copy.wait()
    for span, copy in zip(spans, rows):
        copy.wait()
        out[span, :] = dot(held[span, :], room[...]).astype(bf16)


def grad_kernel(place, grad, weight, keep, send):
    half = keep.shape[1]

    def body(mine, theirs):
        @pl.loop(0, grad.shape[0] // TILE)
        def _(m):
            rows = pl.ds(pl.multiple_of(m * TILE, TILE), TILE)
            send[rows, :] = dot(grad[rows, :], weight[:, theirs : theirs + half])
            keep[rows, :] = dot(grad[rows, :], weight[:, mine : mine + half])

    @pl.when(place[0] == 0)
    def _():
        body(0, half)

    @pl.when(place[0] == 1)
    def _():
        body(half, 0)


def outer_kernel(queries, place, act, act_o, grad, train, train_o, e_out, e_in, out):
    half = train.shape[1]
    lanes = e_in.shape[1]
    count = half // lanes
    first = place[0] == 0
    damp = damping_share * (jnp.sum(e_in[...]) / e_in.size) * (jnp.sum(e_out[...]) / e_out.size)
    e_rows = e_in[pl.ds(pl.multiple_of(place[1] * 8, 8), 8), :]
    low, high = (
        jnp.concatenate([e_rows[r : r + 1, :] for r in range(k * count, (k + 1) * count)], axis=1)
        for k in range(2)
    )
    e_own, e_other = jnp.where(first, low, high), jnp.where(first, high, low)
    e_cols = jnp.transpose(e_out[pl.ds(pl.multiple_of(place[2] * 8, 8), 8), :])
    for start in range(0, half, TILE):
        r = start // lanes
        e_col = jnp.concatenate(
            [
                jnp.where(
                    first,
                    e_cols[:, r + q : r + q + 1],
                    e_cols[:, count + r + q : count + r + q + 1],
                )
                for q in range(TILE // lanes)
            ],
            axis=0,
        )
        total = None
        for a, e_row, t in ((act, e_own, train), (act_o, e_other, train_o)):
            outer = dot_tn(grad[:, start : start + TILE], a[...])
            scaled = (outer / queries / (e_col * e_row + damp)).astype(bf16)
            product = dot_nt(t[...], scaled)
            total = product if total is None else total + product
        out[:, start : start + TILE] = total.astype(bf16)


def back_kernel(place, own, other, b_out, out):
    half = own.shape[1]

    def body(left, right):
        out[...] = (
            dot_nt(left[...], b_out[:, :half]) + dot_nt(right[...], b_out[:, half:])
        ).astype(bf16)

    @pl.when(place[0] == 0)
    def _():
        body(own, other)

    @pl.when(place[0] == 1)
    def _():
        body(other, own)


def call(kernel, args, specs, shapes, out_specs, flops, limit, scratch=()):
    return pl.pallas_call(
        kernel,
        out_shape=shapes,
        in_specs=specs,
        out_specs=out_specs,
        scratch_shapes=scratch,
        compiler_params=pltpu.CompilerParams(vmem_limit_bytes=limit * MIB),
        cost_estimate=pl.CostEstimate(flops=flops, bytes_accessed=4 * MIB, transcendentals=0),
    )(*args)


def summed(pieces):
    return jnp.sum(pieces.astype(f32), axis=0)


def spread(array, n):
    return jnp.broadcast_to(array[None], (n, *array.shape))


def exchanged(array, axes):
    return lax.all_to_all(array, axes, 0, 0, tiled=True)


def per_device(query_act, query_grad, train_rot, basis_in, basis_out, eig_in, eig_out):
    queries, train = query_act.shape[0], train_rot.shape[0]
    width, half = basis_in.shape
    shape = jax.ShapeDtypeStruct
    place = jnp.stack(
        [lax.axis_index("core"), lax.axis_index(CHIPS), lax.axis_index(ROW)]
    ).astype(jnp.int32)
    e_in, e_out = (e.reshape(-1, 128) for e in (eig_in, eig_out))

    act_part = call(
        act_kernel,
        (query_act, basis_in),
        [ANY] * 2,
        shape((queries, half), bf16),
        VMEM,
        2 * queries * width * half,
        58,
        (
            pltpu.VMEM((queries, width), bf16),
            pltpu.VMEM((width, half), bf16),
            pltpu.SemaphoreType.DMA((queries // TILE + 4,)),
        ),
    )
    act_part, query_grad = lax.optimization_barrier((act_part, query_grad))
    keep, send = call(
        grad_kernel,
        (place, query_grad, basis_out),
        [SMEM] + [VMEM] * 2,
        [shape((queries, half), f32)] * 2,
        [VMEM] * 2,
        2 * queries * width * half,
        32,
    )
    grad_part = (keep + lax.ppermute(send, "core", SWAP)).astype(bf16)

    sum_act = summed(exchanged(act_part.reshape(8, -1, half), "y"))
    sum_act, grad_part = lax.optimization_barrier((sum_act, grad_part))
    far_act = lax.ppermute(sum_act.astype(bf16), "z_hi", SWAP).astype(f32)
    sum_grad = summed(exchanged(grad_part.reshape(8, -1, half), NEAR))
    far_act, sum_grad, train_rot = lax.optimization_barrier((far_act, sum_grad, train_rot))
    far_grad = lax.ppermute(sum_grad, "z_a", SWAP)
    train_o = lax.ppermute(train_rot, "core", SWAP)
    act = exchanged(spread((sum_act + far_act).astype(bf16), 8), "y").reshape(queries, half)
    far_grad, act, train_o = lax.optimization_barrier((far_grad, act, train_o))
    act_o = lax.ppermute(act, "core", SWAP)
    grad = exchanged(spread((sum_grad + far_grad).astype(bf16), 8), NEAR).reshape(queries, half)

    partial_inner = call(
        functools.partial(outer_kernel, queries),
        (place, act, act_o, grad, train_rot, train_o, e_out, e_in),
        [SMEM] + [VMEM] * 7,
        shape((train, half), bf16),
        VMEM,
        2 * queries * width * half + 2 * train * width * half,
        32,
    )
    inner_sum = summed(exchanged(partial_inner.reshape(8, -1, half), NEAR))
    inner_sum = inner_sum + lax.ppermute(inner_sum, "z_a", SWAP)
    factor = 1.0 / float(eig_in.shape[0]) ** 0.5
    inner = exchanged(spread((inner_sum * factor).astype(bf16), 8), NEAR).reshape(train, half)
    inner_o = lax.ppermute(inner, "core", SWAP)
    partial_out = call(
        back_kernel,
        (place, inner, inner_o, basis_out),
        [SMEM] + [VMEM] * 3,
        shape((train, half), bf16),
        VMEM,
        2 * train * half * width,
        32,
    )
    return summed(exchanged(partial_out.reshape(16, -1, half), ROW))


def solution(mesh):
    split = Mesh(mesh.devices.reshape(SIZES), ALL)
    placed = (P(None, ROW), P(None, COL), P(None, COL), P(ROW, COL), P(COL, ROW), P(), P())
    return jax.shard_map(
        per_device, mesh=split, in_specs=placed, out_specs=P(ROW, COL), check_vma=False
    )
```

```python
import functools

import jax
import jax.numpy as jnp
import numpy as np
from jax import lax
from jax.experimental import pallas as pl
from jax.experimental.pallas import tpu as pltpu
from jax.sharding import Mesh
from jax.sharding import PartitionSpec as P

ROW = ("z_hi", "y")
CHIPS = ("x", "z_a", "z_b")
COL = (*CHIPS, "core")
ALL = ROW + COL
SIZES = (2, 8, 4, 2, 2, 2)
NEAR = ("x", "z_b")
SWAP = [(0, 1), (1, 0)]
MIB = 1024 * 1024

damping_share = 0.1

bf16 = jnp.bfloat16
f32 = jnp.float32

SMEM = pl.BlockSpec(memory_space=pltpu.SMEM)
VMEM = pl.BlockSpec(memory_space=pltpu.VMEM)
ANY = pl.BlockSpec(memory_space=pl.ANY)


def mixed_groups():
    ids = np.arange(np.prod(SIZES)).reshape(SIZES)
    along_row = ids[..., 0].transpose(0, 2, 3, 4, 1).reshape(-1, 8).tolist()
    along_col = ids[..., 1].transpose(0, 1, 3, 2, 4).reshape(-1, 8).tolist()
    return along_row + along_col


def mixed_pairs():
    ids = np.arange(np.prod(SIZES)).reshape(SIZES)
    to = np.empty_like(ids)
    to[..., 0] = ids[::-1, ..., 0]
    to[..., 1] = ids[:, :, :, ::-1, :, 1]
    return list(zip(ids.reshape(-1).tolist(), to.reshape(-1).tolist()))


def dot(a, b):
    return jnp.dot(a, b, preferred_element_type=f32)


def dot_nt(a, b):
    return lax.dot_general(a, b, (((1,), (1,)), ((), ())), preferred_element_type=f32)


def dot_tn(a, b):
    return lax.dot_general(a, b, (((0,), (0,)), ((), ())), preferred_element_type=f32)


TILE = 256


def damp_kernel(e_in, e_out, damp):
    damp[0] = (
        damping_share * (jnp.sum(e_in[...]) / e_in.size) * (jnp.sum(e_out[...]) / e_out.size)
    )


def rotate_kernel(place, act, grad, b_in, b_out, b_in_o, grad_o, b_out_o, out):
    half = grad.shape[1]

    def body(product):
        @pl.loop(0, out.shape[0] // TILE)
        def _(m):
            product(pl.ds(pl.multiple_of(m * TILE, TILE), TILE))

    def joined(rows):
        out[rows, :half] = dot(act[rows, :], b_in[...]).astype(bf16)
        out[rows, half:] = dot(act[rows, :], b_in_o[...]).astype(bf16)

    def added(rows):
        out[rows, :] = (dot(grad_o[rows, :], b_out_o[...]) + dot(grad[rows, :], b_out[...])).astype(
            bf16
        )

    @pl.when(place[0] == 0)
    def _():
        body(joined)

    @pl.when(place[0] == 1)
    def _():
        body(added)


def outer_kernel(queries, place, damp, own, other, train, train_o, e_out, e_in, out):
    half = train.shape[1]
    lanes = e_in.shape[1]
    e_rows = e_in[pl.ds(pl.multiple_of(place[1] * 8, 8), 8), :]
    e_row = jnp.concatenate([e_rows[r : r + 1, :] for r in range(8)], axis=1)
    e_cols = jnp.transpose(e_out[pl.ds(pl.multiple_of(place[2] * 8, 8), 8), :])

    def body(act, grad, first, left, right):
        for start in range(0, half, TILE):
            outer = dot_tn(grad[:, first + start : first + start + TILE], act[...])
            r = (first + start) // lanes
            e_col = jnp.concatenate([e_cols[:, r + q : r + q + 1] for q in range(TILE // lanes)], axis=0)
            scaled = (outer / queries / (e_col * e_row + damp[0])).astype(bf16)
            out[:, start : start + TILE] = (
                dot_nt(left[...], scaled[:, :half]) + dot_nt(right[...], scaled[:, half:])
            ).astype(bf16)

    @pl.when(place[0] == 0)
    def _():
        body(own, other, 0, train, train_o)

    @pl.when(place[0] == 1)
    def _():
        body(other, own, half, train_o, train)


def back_kernel(place, own, other, b_out, out):
    half = own.shape[1]

    def body(left, right):
        out[...] = (
            dot_nt(left[...], b_out[:, :half]) + dot_nt(right[...], b_out[:, half:])
        ).astype(bf16)

    @pl.when(place[0] == 0)
    def _():
        body(own, other)

    @pl.when(place[0] == 1)
    def _():
        body(other, own)


def call(kernel, args, specs, shapes, out_specs, flops, limit, scratch=()):
    return pl.pallas_call(
        kernel,
        out_shape=shapes,
        in_specs=specs,
        out_specs=out_specs,
        scratch_shapes=scratch,
        compiler_params=pltpu.CompilerParams(vmem_limit_bytes=limit * MIB),
        cost_estimate=pl.CostEstimate(flops=flops, bytes_accessed=4 * MIB, transcendentals=0),
    )(*args)


def summed(pieces):
    return jnp.sum(pieces.astype(f32), axis=0)


def spread(array, n):
    return jnp.broadcast_to(array[None], (n, *array.shape))


def per_device(query_act, query_grad, train_rot, basis_in, basis_out, eig_in, eig_out):
    queries, train = query_act.shape[0], train_rot.shape[0]
    width, half = basis_in.shape
    mixed = functools.partial(
        lax.all_to_all,
        axis_name=ALL,
        split_axis=0,
        concat_axis=0,
        axis_index_groups=mixed_groups(),
        tiled=True,
    )
    near = functools.partial(
        lax.all_to_all, axis_name=NEAR, split_axis=0, concat_axis=0, tiled=True
    )
    shape = jax.ShapeDtypeStruct
    place = jnp.stack(
        [lax.axis_index("core"), lax.axis_index(CHIPS), lax.axis_index(ROW)]
    ).astype(jnp.int32)
    e_in, e_out = (e.reshape(-1, 128) for e in (eig_in, eig_out))

    basis_in_o = lax.ppermute(basis_in, "core", [(1, 0)])
    basis_out_o = lax.ppermute(basis_out, "core", [(0, 1)])
    grad_o = lax.ppermute(query_grad, "core", [(0, 1)])

    damp = call(
        damp_kernel,
        (e_in, e_out),
        [VMEM] * 2,
        shape((1,), f32),
        SMEM,
        6 * 10**9,
        8,
    )
    basis_in_o, basis_out_o, grad_o, damp = lax.optimization_barrier(
        (basis_in_o, basis_out_o, grad_o, damp)
    )
    part = call(
        rotate_kernel,
        (place, query_act, query_grad, basis_in, basis_out, basis_in_o, grad_o, basis_out_o),
        [SMEM] + [VMEM] * 7,
        shape((queries, width), bf16),
        VMEM,
        2 * queries * width * width,
        32,
    )
    eighth = summed(mixed(part.reshape(8, -1, width)))
    eighth, train_rot = lax.optimization_barrier((eighth, train_rot))
    far = lax.ppermute(eighth.astype(bf16), ALL, mixed_pairs()).astype(f32)
    train_o = lax.ppermute(train_rot, "core", SWAP)
    rot = (eighth + far).astype(bf16)
    rot, train_o = lax.optimization_barrier((rot, train_o))
    own = mixed(spread(rot, 8)).reshape(queries, width)
    other = lax.ppermute(own, "core", SWAP)

    partial_inner = call(
        functools.partial(outer_kernel, queries),
        (place, damp, own, other, train_rot, train_o, e_out, e_in),
        [SMEM] * 2 + [VMEM] * 6,
        shape((train, half), bf16),
        VMEM,
        2 * queries * width * half + 2 * train * width * half,
        32,
    )
    inner_sum = summed(near(partial_inner.reshape(8, -1, half)))
    inner_sum = inner_sum + lax.ppermute(inner_sum, "z_a", SWAP)
    factor = 1.0 / float(eig_in.shape[0]) ** 0.5
    inner = near(spread((inner_sum * factor).astype(bf16), 8)).reshape(train, half)
    inner_o = lax.ppermute(inner, "core", SWAP)
    partial_out = call(
        back_kernel,
        (place, inner, inner_o, basis_out),
        [SMEM] + [VMEM] * 3,
        shape((train, half), bf16),
        VMEM,
        2 * train * half * width,
        32,
    )
    return summed(lax.all_to_all(partial_out.reshape(16, -1, half), ROW, 0, 0, tiled=True))


def solution(mesh):
    split = Mesh(mesh.devices.reshape(SIZES), ALL)
    placed = (P(None, ROW), P(None, COL), P(None, COL), P(ROW, COL), P(COL, ROW), P(), P())
    return jax.shard_map(
        per_device, mesh=split, in_specs=placed, out_specs=P(ROW, COL), check_vma=False
    )
```

```python
import functools

import jax
import jax.numpy as jnp
from jax import lax
from jax.experimental import pallas as pl
from jax.experimental.pallas import tpu as pltpu
from jax.sharding import Mesh
from jax.sharding import PartitionSpec as P

ROW = ("z_hi", "y")
CHIPS = ("x", "z_a", "z_b")
COL = (*CHIPS, "core")
ALL = ROW + COL
SIZES = (2, 8, 4, 2, 2, 2)
NEAR = ("x", "z_b")
SWAP = [(0, 1), (1, 0)]
MIB = 1024 * 1024

damping_share = 0.1

bf16 = jnp.bfloat16
f32 = jnp.float32

SMEM = pl.BlockSpec(memory_space=pltpu.SMEM)
VMEM = pl.BlockSpec(memory_space=pltpu.VMEM)
ANY = pl.BlockSpec(memory_space=pl.ANY)


def dot(a, b):
    return jnp.dot(a, b, preferred_element_type=f32)


def dot_nt(a, b):
    return lax.dot_general(a, b, (((1,), (1,)), ((), ())), preferred_element_type=f32)


def dot_tn(a, b):
    return lax.dot_general(a, b, (((0,), (0,)), ((), ())), preferred_element_type=f32)


TILE = 256


def act_kernel(act, weight, out, held, room, sems):
    steps = act.shape[0] // TILE
    pieces = sems.shape[0] - steps
    depth = weight.shape[0] // pieces
    loads = [
        pltpu.make_async_copy(
            weight.at[pl.ds(p * depth, depth)], room.at[pl.ds(p * depth, depth)], sems.at[steps + p]
        )
        for p in range(pieces)
    ]
    spans = [pl.ds(m * TILE, TILE) for m in range(steps)]
    rows = [
        pltpu.make_async_copy(act.at[span], held.at[span], sems.at[m])
        for m, span in enumerate(spans)
    ]
    for copy in loads + rows:
        copy.start()
    for copy in loads:
        copy.wait()
    for span, copy in zip(spans, rows):
        copy.wait()
        out[span, :] = dot(held[span, :], room[...]).astype(bf16)


def grad_kernel(place, grad, weight, keep, send):
    half = keep.shape[1]

    def body(mine, theirs):
        @pl.loop(0, grad.shape[0] // TILE)
        def _(m):
            rows = pl.ds(pl.multiple_of(m * TILE, TILE), TILE)
            send[rows, :] = dot(grad[rows, :], weight[:, theirs : theirs + half])
            keep[rows, :] = dot(grad[rows, :], weight[:, mine : mine + half])

    @pl.when(place[0] == 0)
    def _():
        body(0, half)

    @pl.when(place[0] == 1)
    def _():
        body(half, 0)


def outer_kernel(queries, place, act, act_o, grad, train, train_o, e_out, e_in, out):
    half = train.shape[1]
    lanes = e_in.shape[1]
    count = half // lanes
    first = place[0] == 0
    damp = damping_share * (jnp.sum(e_in[...]) / e_in.size) * (jnp.sum(e_out[...]) / e_out.size)
    e_rows = e_in[pl.ds(pl.multiple_of(place[1] * 8, 8), 8), :]
    low, high = (
        jnp.concatenate([e_rows[r : r + 1, :] for r in range(k * count, (k + 1) * count)], axis=1)
        for k in range(2)
    )
    e_own, e_other = jnp.where(first, low, high), jnp.where(first, high, low)
    e_cols = jnp.transpose(e_out[pl.ds(pl.multiple_of(place[2] * 8, 8), 8), :])
    for start in range(0, half, TILE):
        r = start // lanes
        e_col = jnp.concatenate(
            [
                jnp.where(
                    first,
                    e_cols[:, r + q : r + q + 1],
                    e_cols[:, count + r + q : count + r + q + 1],
                )
                for q in range(TILE // lanes)
            ],
            axis=0,
        )
        total = None
        for a, e_row, t in ((act, e_own, train), (act_o, e_other, train_o)):
            outer = dot_tn(grad[:, start : start + TILE], a[...])
            scaled = (outer / queries / (e_col * e_row + damp)).astype(bf16)
            product = dot_nt(t[...], scaled)
            total = product if total is None else total + product
        out[:, start : start + TILE] = total.astype(bf16)


def back_kernel(place, own, other, b_out, out):
    half = own.shape[1]

    def body(left, right):
        out[...] = (
            dot_nt(left[...], b_out[:, :half]) + dot_nt(right[...], b_out[:, half:])
        ).astype(bf16)

    @pl.when(place[0] == 0)
    def _():
        body(own, other)

    @pl.when(place[0] == 1)
    def _():
        body(other, own)


def call(kernel, args, specs, shapes, out_specs, flops, limit, scratch=()):
    return pl.pallas_call(
        kernel,
        out_shape=shapes,
        in_specs=specs,
        out_specs=out_specs,
        scratch_shapes=scratch,
        compiler_params=pltpu.CompilerParams(vmem_limit_bytes=limit * MIB),
        cost_estimate=pl.CostEstimate(flops=flops, bytes_accessed=4 * MIB, transcendentals=0),
    )(*args)


def summed(pieces):
    return jnp.sum(pieces.astype(f32), axis=0)


def spread(array, n):
    return jnp.broadcast_to(array[None], (n, *array.shape))


def exchanged(array, axes):
    return lax.all_to_all(array, axes, 0, 0, tiled=True)


def per_device(query_act, query_grad, train_rot, basis_in, basis_out, eig_in, eig_out):
    queries, train = query_act.shape[0], train_rot.shape[0]
    width, half = basis_in.shape
    shape = jax.ShapeDtypeStruct
    place = jnp.stack(
        [lax.axis_index("core"), lax.axis_index(CHIPS), lax.axis_index(ROW)]
    ).astype(jnp.int32)
    e_in, e_out = (e.reshape(-1, 128) for e in (eig_in, eig_out))

    act_part = call(
        act_kernel,
        (query_act, basis_in),
        [ANY] * 2,
        shape((queries, half), bf16),
        VMEM,
        2 * queries * width * half,
        58,
        (
            pltpu.VMEM((queries, width), bf16),
            pltpu.VMEM((width, half), bf16),
            pltpu.SemaphoreType.DMA((queries // TILE + 4,)),
        ),
    )
    act_part, query_grad = lax.optimization_barrier((act_part, query_grad))
    keep, send = call(
        grad_kernel,
        (place, query_grad, basis_out),
        [SMEM] + [VMEM] * 2,
        [shape((queries, half), f32)] * 2,
        [VMEM] * 2,
        2 * queries * width * half,
        32,
    )
    grad_part = (keep + lax.ppermute(send, "core", SWAP)).astype(bf16)

    sum_act = summed(exchanged(act_part.reshape(8, -1, half), "y"))
    sum_act, grad_part = lax.optimization_barrier((sum_act, grad_part))
    sum_grad = summed(exchanged(grad_part.reshape(8, -1, half), NEAR))
    sum_act, sum_grad, train_rot = lax.optimization_barrier((sum_act, sum_grad, train_rot))
    far_act = lax.ppermute(sum_act.astype(bf16), "z_hi", SWAP).astype(f32)
    far_grad = lax.ppermute(sum_grad.astype(bf16), "z_a", SWAP).astype(f32)
    act_sum, grad_sum = (sum_act + far_act).astype(bf16), (sum_grad + far_grad).astype(bf16)
    act_sum, grad_sum, train_rot = lax.optimization_barrier((act_sum, grad_sum, train_rot))
    act = exchanged(spread(act_sum, 8), "y").reshape(queries, half)
    grad_sum, act, train_rot = lax.optimization_barrier((grad_sum, act, train_rot))
    act_o = lax.ppermute(act, "core", SWAP)
    train_rot = train_rot.reshape(2, 8, -1, half).swapaxes(0, 1).reshape(train, half)
    train_o = lax.ppermute(train_rot, "core", SWAP)
    grad = exchanged(spread(grad_sum, 8), NEAR).reshape(queries, half)

    partial_inner = call(
        functools.partial(outer_kernel, queries),
        (place, act, act_o, grad, train_rot, train_o, e_out, e_in),
        [SMEM] + [VMEM] * 7,
        shape((train, half), bf16),
        VMEM,
        2 * queries * width * half + 2 * train * width * half,
        32,
    )
    inner_sum = summed(exchanged(partial_inner.reshape(8, -1, half), NEAR))
    inner_sum = inner_sum + lax.ppermute(inner_sum, "z_a", SWAP)
    factor = 1.0 / float(eig_in.shape[0]) ** 0.5
    inner = exchanged(spread((inner_sum * factor).astype(bf16), 8), NEAR).reshape(train, half)
    inner_o = lax.ppermute(inner, "core", SWAP)
    partial_out = call(
        back_kernel,
        (place, inner, inner_o, basis_out),
        [SMEM] + [VMEM] * 3,
        shape((train, half), bf16),
        VMEM,
        2 * train * half * width,
        32,
    )
    rows = summed(exchanged(partial_out.reshape(8, -1, half), "y")).reshape(2, -1, half)
    z = lax.axis_index("z_hi")
    mine, theirs = (lax.dynamic_index_in_dim(rows, i, 0, keepdims=False) for i in (z, 1 - z))
    return mine + lax.ppermute(theirs, "z_hi", SWAP)


def solution(mesh):
    split = Mesh(mesh.devices.reshape(SIZES), ALL)
    placed = (P(None, ROW), P(None, COL), P(None, COL), P(ROW, COL), P(COL, ROW), P(), P())
    return jax.shard_map(
        per_device, mesh=split, in_specs=placed, out_specs=P(ROW, COL), check_vma=False
    )
```

```python
import functools

import jax
import jax.numpy as jnp
import numpy as np
from jax import lax
from jax.experimental import pallas as pl
from jax.experimental.pallas import tpu as pltpu
from jax.sharding import Mesh
from jax.sharding import PartitionSpec as P

ROW = ("z_hi", "y")
CHIPS = ("x", "z_a", "z_b")
COL = (*CHIPS, "core")
ALL = ROW + COL
SIZES = (2, 8, 4, 2, 2, 2)
NEAR = ("x", "z_b")
SWAP = [(0, 1), (1, 0)]
MIB = 1024 * 1024

damping_share = 0.1

bf16 = jnp.bfloat16
f32 = jnp.float32

SMEM = pl.BlockSpec(memory_space=pltpu.SMEM)
VMEM = pl.BlockSpec(memory_space=pltpu.VMEM)
ANY = pl.BlockSpec(memory_space=pl.ANY)


def device_ids():
    return np.arange(np.prod(SIZES)).reshape(2, 8, 2, 2, 4, 2)


def mixed_groups():
    ids = device_ids()
    along_row = ids[..., 0].transpose(0, 2, 3, 4, 1).reshape(-1, 8).tolist()
    along_col = ids[..., 1].reshape(-1, 8).tolist()
    return along_row + along_col


def mixed_pairs():
    ids = device_ids()
    to = np.empty_like(ids)
    to[..., 0] = ids[::-1, ..., 0]
    to[..., 1] = ids[:, :, ::-1, :, :, 1]
    return list(zip(ids.reshape(-1).tolist(), to.reshape(-1).tolist()))


def dot(a, b):
    return jnp.dot(a, b, preferred_element_type=f32)


def dot_nt(a, b):
    return lax.dot_general(a, b, (((1,), (1,)), ((), ())), preferred_element_type=f32)


def dot_tn(a, b):
    return lax.dot_general(a, b, (((0,), (0,)), ((), ())), preferred_element_type=f32)


TILE = 256


def first_kernel(core, token):
    token[0] = core[0]


def rotate_kernel(core, act, grad, b_in, b_out, b_in_o, grad_o, b_out_o, out):
    half = grad.shape[1]

    def body(product):
        @pl.loop(0, out.shape[0] // TILE)
        def _(m):
            product(pl.ds(pl.multiple_of(m * TILE, TILE), TILE))

    def joined(rows):
        out[rows, :half] = dot(act[rows, :], b_in[...]).astype(bf16)
        out[rows, half:] = dot(act[rows, :], b_in_o[...]).astype(bf16)

    def added(rows):
        out[rows, :] = (dot(grad_o[rows, :], b_out_o[...]) + dot(grad[rows, :], b_out[...])).astype(
            bf16
        )

    @pl.when(core[0] == 0)
    def _():
        body(joined)

    @pl.when(core[0] == 1)
    def _():
        body(added)


def outer_kernel(queries, place, token, own, other, train, train_o, e_out, e_in, out):
    half = train.shape[1]
    lanes = e_in.shape[1]
    damp = damping_share * (jnp.sum(e_in[...]) / e_in.size) * (jnp.sum(e_out[...]) / e_out.size)
    e_rows = e_in[pl.ds(pl.multiple_of(place[1] * 8, 8), 8), :]
    e_row = jnp.concatenate([e_rows[r : r + 1, :] for r in range(8)], axis=1)
    e_cols = jnp.transpose(e_out[pl.ds(pl.multiple_of(place[2] * 8, 8), 8), :])

    def body(act, grad, first, left, right):
        for start in range(0, half, TILE):
            outer = dot_tn(grad[:, first + start : first + start + TILE], act[...])
            r = (first + start) // lanes
            e_col = jnp.concatenate([e_cols[:, r + q : r + q + 1] for q in range(TILE // lanes)], axis=0)
            scaled = (outer / queries / (e_col * e_row + damp)).astype(bf16)
            out[:, start : start + TILE] = (
                dot_nt(left[...], scaled[:, :half]) + dot_nt(right[...], scaled[:, half:])
            ).astype(bf16)

    @pl.when(place[0] == 0)
    def _():
        body(own, other, 0, train, train_o)

    @pl.when(place[0] == 1)
    def _():
        body(other, own, half, train_o, train)


def back_kernel(core, own, other, b_out, out):
    half = own.shape[1]

    def body(left, right):
        out[...] = (
            dot_nt(left[...], b_out[:, :half]) + dot_nt(right[...], b_out[:, half:])
        ).astype(bf16)

    @pl.when(core[0] == 0)
    def _():
        body(own, other)

    @pl.when(core[0] == 1)
    def _():
        body(other, own)


def call(kernel, args, specs, shapes, out_specs, flops, limit, scratch=()):
    return pl.pallas_call(
        kernel,
        out_shape=shapes,
        in_specs=specs,
        out_specs=out_specs,
        scratch_shapes=scratch,
        compiler_params=pltpu.CompilerParams(vmem_limit_bytes=limit * MIB),
        cost_estimate=pl.CostEstimate(flops=flops, bytes_accessed=4 * MIB, transcendentals=0),
    )(*args)


def summed(pieces):
    return jnp.sum(pieces.astype(f32), axis=0)


def spread(array, n):
    return jnp.broadcast_to(array[None], (n, *array.shape))


def per_device(query_act, query_grad, train_rot, basis_in, basis_out, eig_in, eig_out):
    queries, train = query_act.shape[0], train_rot.shape[0]
    width, half = basis_in.shape
    mixed = functools.partial(
        lax.all_to_all,
        axis_name=ALL,
        split_axis=0,
        concat_axis=0,
        axis_index_groups=mixed_groups(),
        tiled=True,
    )
    near = functools.partial(
        lax.all_to_all, axis_name=NEAR, split_axis=0, concat_axis=0, tiled=True
    )
    shape = jax.ShapeDtypeStruct
    place = jnp.stack(
        [lax.axis_index("core"), lax.axis_index(CHIPS), lax.axis_index(ROW)]
    ).astype(jnp.int32)
    core = lax.axis_index("core").astype(jnp.int32).reshape(1)
    e_in, e_out = (e.reshape(-1, 128) for e in (eig_in, eig_out))

    basis_in_o = lax.ppermute(basis_in, "core", [(1, 0)])
    basis_out_o = lax.ppermute(basis_out, "core", [(0, 1)])
    grad_o = lax.ppermute(query_grad, "core", [(0, 1)])

    token = call(
        first_kernel,
        (core,),
        [SMEM],
        shape((1,), jnp.int32),
        SMEM,
        6 * 10**9,
        8,
    )
    basis_in_o, basis_out_o, grad_o, token = lax.optimization_barrier(
        (basis_in_o, basis_out_o, grad_o, token)
    )
    part = call(
        rotate_kernel,
        (place, query_act, query_grad, basis_in, basis_out, basis_in_o, grad_o, basis_out_o),
        [SMEM] + [VMEM] * 7,
        shape((queries, width), bf16),
        VMEM,
        2 * queries * width * width,
        32,
    )
    eighth = summed(mixed(part.reshape(8, -1, width)))
    eighth, train_rot = lax.optimization_barrier((eighth, train_rot))
    far = lax.ppermute(eighth.astype(bf16), ALL, mixed_pairs()).astype(f32)
    train_o = lax.ppermute(train_rot, "core", SWAP)
    rot = (eighth + far).astype(bf16)
    rot, train_o = lax.optimization_barrier((rot, train_o))
    own = mixed(spread(rot, 8)).reshape(queries, width)
    other = lax.ppermute(own, "core", SWAP)

    partial_inner = call(
        functools.partial(outer_kernel, queries),
        (place, token, own, other, train_rot, train_o, e_out, e_in),
        [SMEM] * 2 + [VMEM] * 6,
        shape((train, half), bf16),
        VMEM,
        2 * queries * width * half + 2 * train * width * half,
        32,
    )
    inner_sum = summed(near(partial_inner.reshape(8, -1, half)))
    inner_sum = inner_sum + lax.ppermute(inner_sum, "z_a", SWAP)
    factor = 1.0 / float(eig_in.shape[0]) ** 0.5
    inner = near(spread((inner_sum * factor).astype(bf16), 8)).reshape(train, half)
    inner_o = lax.ppermute(inner, "core", SWAP)
    partial_out = call(
        back_kernel,
        (core, inner, inner_o, basis_out),
        [SMEM] + [VMEM] * 3,
        shape((train, half), bf16),
        VMEM,
        2 * train * half * width,
        32,
    )
    return summed(lax.all_to_all(partial_out.reshape(16, -1, half), ROW, 0, 0, tiled=True))


def solution(mesh):
    split = Mesh(mesh.devices.reshape(SIZES), ALL)
    placed = (P(None, ROW), P(None, COL), P(None, COL), P(ROW, COL), P(COL, ROW), P(), P())
    return jax.shard_map(
        per_device, mesh=split, in_specs=placed, out_specs=P(ROW, COL), check_vma=False
    )
```

```python
import functools

import jax
import jax.numpy as jnp
import numpy as np
from jax import lax
from jax.experimental import pallas as pl
from jax.experimental.pallas import tpu as pltpu
from jax.sharding import Mesh
from jax.sharding import PartitionSpec as P

ROW = ("z_hi", "y")
CHIPS = ("x", "z_a", "z_b")
COL = (*CHIPS, "core")
ALL = ROW + COL
SIZES = (2, 8, 4, 2, 2, 2)
NEAR = ("x", "z_b")
SWAP = [(0, 1), (1, 0)]
MIB = 1024 * 1024

damping_share = 0.1

bf16 = jnp.bfloat16
f32 = jnp.float32

SMEM = pl.BlockSpec(memory_space=pltpu.SMEM)
VMEM = pl.BlockSpec(memory_space=pltpu.VMEM)
ANY = pl.BlockSpec(memory_space=pl.ANY)


def parity():
    z_hi, y, x, _, z_b = np.indices(SIZES[:-1])
    return (z_hi + y + x + z_b) % 2


def role_ids():
    ids = np.arange(np.prod(SIZES)).reshape(SIZES)
    first = parity()[..., None]
    return np.take_along_axis(ids, np.concatenate([first, 1 - first], axis=-1), axis=-1)


def mixed_groups():
    ids = role_ids()
    along_row = ids[..., 0].transpose(0, 2, 3, 4, 1).reshape(-1, 8).tolist()
    along_col = ids[..., 1].transpose(0, 1, 3, 2, 4).reshape(-1, 8).tolist()
    return along_row + along_col


def mixed_pairs():
    ids = role_ids()
    to = np.empty_like(ids)
    to[..., 0] = ids[::-1, ..., 0]
    to[..., 1] = ids[:, :, :, ::-1, :, 1]
    return list(zip(ids.reshape(-1).tolist(), to.reshape(-1).tolist()))


def final_groups():
    ids = np.arange(np.prod(SIZES)).reshape(2, 2, 2, 2, -1)
    return ids.transpose(3, 2, 1, 0, 4).reshape(16, -1).T.tolist()


def role_pairs(source):
    ids = role_ids().reshape(-1, 2)
    return list(zip(ids[:, source].tolist(), ids[:, 1 - source].tolist()))


def dot(a, b):
    return jnp.dot(a, b, preferred_element_type=f32)


def dot_nt(a, b):
    return lax.dot_general(a, b, (((1,), (1,)), ((), ())), preferred_element_type=f32)


def dot_tn(a, b):
    return lax.dot_general(a, b, (((0,), (0,)), ((), ())), preferred_element_type=f32)


def first_kernel(core, token):
    token[0] = core[0]


def rotate_kernel(place, act, grad, b_in, b_out, b_in_o, grad_o, b_out_o, out):
    half = grad.shape[1]

    def joined(low, high):
        out[:, :half] = dot(act[...], low[...]).astype(bf16)
        out[:, half:] = dot(act[...], high[...]).astype(bf16)

    @pl.when((place[3] == 0) & (place[0] == 0))
    def _():
        joined(b_in, b_in_o)

    @pl.when((place[3] == 0) & (place[0] == 1))
    def _():
        joined(b_in_o, b_in)

    @pl.when(place[3] == 1)
    def _():
        out[...] = (dot(grad_o[...], b_out_o[...]) + dot(grad[...], b_out[...])).astype(bf16)


def outer_kernel(queries, place, token, own, other, train, train_o, e_out, e_in, out):
    half = train.shape[1]
    lanes = e_in.shape[1]
    damp = damping_share * (jnp.sum(e_in[...]) / e_in.size) * (jnp.sum(e_out[...]) / e_out.size)
    e_rows = e_in[pl.ds(pl.multiple_of(place[1] * 8, 8), 8), :]
    e_row = jnp.concatenate([e_rows[r : r + 1, :] for r in range(8)], axis=1)
    e_cols = jnp.transpose(e_out[pl.ds(pl.multiple_of(place[2] * 8, 8), 8), :])

    def body(act, grad, first, left, right):
        outer = dot_tn(grad[:, first : first + half], act[...])
        r = first // lanes
        e_col = jnp.concatenate([e_cols[:, r + q : r + q + 1] for q in range(half // lanes)], axis=0)
        scaled = (outer / ((e_col * queries) * e_row + damp * queries)).astype(bf16)
        out[...] = (
            dot_nt(left[...], scaled[:, :half]) + dot_nt(right[...], scaled[:, half:])
        ).astype(bf16)

    for role, (act, grad) in enumerate(((own, other), (other, own))):
        for core, (left, right) in enumerate(((train, train_o), (train_o, train))):

            @pl.when((place[3] == role) & (place[0] == core))
            def _():
                body(act, grad, core * half, left, right)


def back_kernel(core, own, other, b_out, out):
    half = own.shape[1]

    def body(left, right):
        out[...] = (
            dot_nt(left[...], b_out[:, :half]) + dot_nt(right[...], b_out[:, half:])
        ).astype(bf16)

    @pl.when(core[0] == 0)
    def _():
        body(own, other)

    @pl.when(core[0] == 1)
    def _():
        body(other, own)


def call(kernel, args, specs, shapes, out_specs, flops, limit, scratch=()):
    return pl.pallas_call(
        kernel,
        out_shape=shapes,
        in_specs=specs,
        out_specs=out_specs,
        scratch_shapes=scratch,
        compiler_params=pltpu.CompilerParams(vmem_limit_bytes=limit * MIB),
        cost_estimate=pl.CostEstimate(flops=flops, bytes_accessed=4 * MIB, transcendentals=0),
    )(*args)


def summed(pieces):
    return jnp.sum(pieces.astype(f32), axis=0)


def spread(array, n):
    return jnp.broadcast_to(array[None], (n, *array.shape))


def per_device(query_act, query_grad, train_rot, basis_in, basis_out, eig_in, eig_out):
    queries, train = query_act.shape[0], train_rot.shape[0]
    width, half = basis_in.shape
    mixed = functools.partial(
        lax.all_to_all,
        axis_name=ALL,
        split_axis=0,
        concat_axis=0,
        axis_index_groups=mixed_groups(),
        tiled=True,
    )
    near = functools.partial(
        lax.all_to_all, axis_name=NEAR, split_axis=0, concat_axis=0, tiled=True
    )
    shape = jax.ShapeDtypeStruct
    spots = [lax.axis_index(axis) for axis in ("z_hi", "y", "x", "z_b", "core")]
    place = jnp.stack(
        [spots[-1], lax.axis_index(CHIPS), lax.axis_index(ROW), sum(spots) % 2]
    ).astype(jnp.int32)
    core = lax.axis_index("core").astype(jnp.int32).reshape(1)
    e_in, e_out = (e.reshape(-1, 128) for e in (eig_in, eig_out))

    basis_in_o = lax.ppermute(basis_in, ALL, role_pairs(1))
    basis_out_o = lax.ppermute(basis_out, ALL, role_pairs(0))
    grad_o = lax.ppermute(query_grad, ALL, role_pairs(0))

    token = call(
        first_kernel,
        (core,),
        [SMEM],
        shape((1,), jnp.int32),
        SMEM,
        6 * 10**9,
        8,
    )
    basis_in_o, basis_out_o, grad_o, token = lax.optimization_barrier(
        (basis_in_o, basis_out_o, grad_o, token)
    )
    part = call(
        rotate_kernel,
        (place, query_act, query_grad, basis_in, basis_out, basis_in_o, grad_o, basis_out_o),
        [SMEM] + [VMEM] * 7,
        shape((queries, width), bf16),
        VMEM,
        2 * queries * width * width,
        32,
    )
    eighth = summed(mixed(part.reshape(8, -1, width)))
    eighth, train_rot = lax.optimization_barrier((eighth, train_rot))
    far = lax.ppermute(eighth.astype(bf16), ALL, mixed_pairs()).astype(f32)
    train_rot = train_rot.reshape(2, 2, 2, 2, -1, half).transpose(3, 2, 1, 0, 4, 5)
    train_rot = train_rot.reshape(train, half)
    train_o = lax.ppermute(train_rot, "core", SWAP)
    rot = (eighth + far).astype(bf16)
    rot, train_o = lax.optimization_barrier((rot, train_o))
    own = mixed(spread(rot, 8)).reshape(queries, width)
    other = lax.ppermute(own, "core", SWAP)

    partial_inner = call(
        functools.partial(outer_kernel, queries),
        (place, token, own, other, train_rot, train_o, e_out, e_in),
        [SMEM] * 2 + [VMEM] * 6,
        shape((train, half), bf16),
        VMEM,
        2 * queries * width * half + 2 * train * width * half,
        32,
    )
    inner_sum = summed(near(partial_inner.reshape(8, -1, half)))
    inner_sum = inner_sum + lax.ppermute(inner_sum, "z_a", SWAP)
    factor = 1.0 / float(eig_in.shape[0]) ** 0.5
    inner = near(spread((inner_sum * factor).astype(bf16), 8)).reshape(train, half)
    inner_o = lax.ppermute(inner, "core", SWAP)
    partial_out = call(
        back_kernel,
        (core, inner, inner_o, basis_out),
        [SMEM] + [VMEM] * 3,
        shape((train, half), bf16),
        VMEM,
        2 * train * half * width,
        32,
    )
    final = lax.all_to_all(
        partial_out.reshape(16, -1, half), ALL, 0, 0, axis_index_groups=final_groups(), tiled=True
    )
    return summed(final)


def solution(mesh):
    split = Mesh(mesh.devices.reshape(SIZES), ALL)
    placed = (P(None, ROW), P(None, COL), P(None, COL), P(ROW, COL), P(COL, ROW), P(), P())
    return jax.shard_map(
        per_device, mesh=split, in_specs=placed, out_specs=P(ROW, COL), check_vma=False
    )
```

```python
import functools

import jax
import jax.numpy as jnp
import numpy as np
from jax import lax
from jax.experimental import pallas as pl
from jax.experimental.pallas import tpu as pltpu
from jax.sharding import Mesh
from jax.sharding import PartitionSpec as P

ROW = ("z_hi", "y")
CHIPS = ("x", "z_a", "z_b")
COL = (*CHIPS, "core")
ALL = ROW + COL
SIZES = (2, 8, 4, 2, 2, 2)
NEAR = ("x", "z_b")
SWAP = [(0, 1), (1, 0)]
MIB = 1024 * 1024

damping_share = 0.1

bf16 = jnp.bfloat16
f32 = jnp.float32

SMEM = pl.BlockSpec(memory_space=pltpu.SMEM)
VMEM = pl.BlockSpec(memory_space=pltpu.VMEM)
ANY = pl.BlockSpec(memory_space=pl.ANY)


def parity():
    z_hi, y, x, _, z_b = np.indices(SIZES[:-1])
    return (z_hi + y + x + z_b) % 2


def role_ids():
    ids = np.arange(np.prod(SIZES)).reshape(SIZES)
    first = parity()[..., None]
    return np.take_along_axis(ids, np.concatenate([first, 1 - first], axis=-1), axis=-1)


def mixed_groups():
    ids = role_ids()
    along_row = ids[..., 0].transpose(0, 2, 3, 4, 1).reshape(-1, 8).tolist()
    along_col = ids[..., 1].transpose(0, 1, 3, 2, 4).reshape(-1, 8).tolist()
    return along_row + along_col


def mixed_pairs():
    ids = role_ids()
    to = np.empty_like(ids)
    to[..., 0] = ids[::-1, ..., 0]
    to[..., 1] = ids[:, :, :, ::-1, :, 1]
    return list(zip(ids.reshape(-1).tolist(), to.reshape(-1).tolist()))


def role_pairs(source):
    ids = role_ids().reshape(-1, 2)
    return list(zip(ids[:, source].tolist(), ids[:, 1 - source].tolist()))


def dot(a, b):
    return jnp.dot(a, b, preferred_element_type=f32)


def dot_nt(a, b):
    return lax.dot_general(a, b, (((1,), (1,)), ((), ())), preferred_element_type=f32)


def dot_tn(a, b):
    return lax.dot_general(a, b, (((0,), (0,)), ((), ())), preferred_element_type=f32)


def first_kernel(core, token):
    token[0] = core[0]


def rotate_kernel(place, act, grad, b_in, b_out, b_in_o, b_out_o, grad_o, out, held, sem):
    half = grad.shape[1]

    def joined(low, high):
        out[:, :half] = dot(act[...], low[...]).astype(bf16)
        out[:, half:] = dot(act[...], high[...]).astype(bf16)

    @pl.when((place[3] == 0) & (place[0] == 0))
    def _():
        joined(b_in, b_in_o)

    @pl.when((place[3] == 0) & (place[0] == 1))
    def _():
        joined(b_in_o, b_in)

    @pl.when(place[3] == 1)
    def _():
        load = pltpu.make_async_copy(grad_o, held, sem)
        load.start()
        load.wait()
        out[...] = (dot(held[...], b_out_o[...]) + dot(grad[...], b_out[...])).astype(bf16)


def outer_kernel(queries, place, token, own, other, train, train_o, e_out, e_in, out):
    half = train.shape[1]
    lanes = e_in.shape[1]
    damp = damping_share * (jnp.sum(e_in[...]) / e_in.size) * (jnp.sum(e_out[...]) / e_out.size)
    e_rows = e_in[pl.ds(pl.multiple_of(place[1] * 8, 8), 8), :]
    e_row = jnp.concatenate([e_rows[r : r + 1, :] for r in range(8)], axis=1)
    e_cols = jnp.transpose(e_out[pl.ds(pl.multiple_of(place[2] * 8, 8), 8), :])

    def body(act, grad, first, left, right):
        outer = dot_tn(grad[:, first : first + half], act[...])
        r = first // lanes
        e_col = jnp.concatenate([e_cols[:, r + q : r + q + 1] for q in range(half // lanes)], axis=0)
        scaled = (outer / ((e_col * queries) * e_row + damp * queries)).astype(bf16)
        out[...] = (
            dot_nt(left[...], scaled[:, :half]) + dot_nt(right[...], scaled[:, half:])
        ).astype(bf16)

    for role, (act, grad) in enumerate(((own, other), (other, own))):
        for core, (left, right) in enumerate(((train, train_o), (train_o, train))):

            @pl.when((place[3] == role) & (place[0] == core))
            def _():
                body(act, grad, core * half, left, right)


def back_kernel(core, own, other, b_out, out):
    half = own.shape[1]

    def body(left, right):
        out[...] = (
            dot_nt(left[...], b_out[:, :half]) + dot_nt(right[...], b_out[:, half:])
        ).astype(bf16)

    @pl.when(core[0] == 0)
    def _():
        body(own, other)

    @pl.when(core[0] == 1)
    def _():
        body(other, own)


def call(kernel, args, specs, shapes, out_specs, flops, limit, scratch=()):
    return pl.pallas_call(
        kernel,
        out_shape=shapes,
        in_specs=specs,
        out_specs=out_specs,
        scratch_shapes=scratch,
        compiler_params=pltpu.CompilerParams(vmem_limit_bytes=limit * MIB),
        cost_estimate=pl.CostEstimate(flops=flops, bytes_accessed=4 * MIB, transcendentals=0),
    )(*args)


def summed(pieces):
    return jnp.sum(pieces.astype(f32), axis=0)


def spread(array, n):
    return jnp.broadcast_to(array[None], (n, *array.shape))


def per_device(query_act, query_grad, train_rot, basis_in, basis_out, eig_in, eig_out):
    queries, train = query_act.shape[0], train_rot.shape[0]
    width, half = basis_in.shape
    mixed = functools.partial(
        lax.all_to_all,
        axis_name=ALL,
        split_axis=0,
        concat_axis=0,
        axis_index_groups=mixed_groups(),
        tiled=True,
    )
    near = functools.partial(
        lax.all_to_all, axis_name=NEAR, split_axis=0, concat_axis=0, tiled=True
    )
    shape = jax.ShapeDtypeStruct
    spots = [lax.axis_index(axis) for axis in ("z_hi", "y", "x", "z_b", "core")]
    place = jnp.stack(
        [spots[-1], lax.axis_index(CHIPS), lax.axis_index(ROW), sum(spots) % 2]
    ).astype(jnp.int32)
    core = lax.axis_index("core").astype(jnp.int32).reshape(1)
    e_in, e_out = (e.reshape(-1, 128) for e in (eig_in, eig_out))

    basis_in_o = lax.ppermute(basis_in, ALL, role_pairs(1))
    basis_out_o = lax.ppermute(basis_out, ALL, role_pairs(0))
    grad_o = lax.ppermute(query_grad, ALL, role_pairs(0))

    token = call(
        first_kernel,
        (core,),
        [SMEM],
        shape((1,), jnp.int32),
        SMEM,
        6 * 10**9,
        8,
    )
    basis_in_o, basis_out_o, grad_o, token = lax.optimization_barrier(
        (basis_in_o, basis_out_o, grad_o, token)
    )
    part = call(
        rotate_kernel,
        (place, query_act, query_grad, basis_in, basis_out, basis_in_o, basis_out_o, grad_o),
        [SMEM] + [VMEM] * 6 + [ANY],
        shape((queries, width), bf16),
        VMEM,
        2 * queries * width * width,
        32,
        (pltpu.VMEM((queries, half), bf16), pltpu.SemaphoreType.DMA),
    )
    eighth = summed(mixed(part.reshape(8, -1, width)))
    eighth, train_rot = lax.optimization_barrier((eighth, train_rot))
    far = lax.ppermute(eighth.astype(bf16), ALL, mixed_pairs()).astype(f32)
    train_o = lax.ppermute(train_rot, "core", SWAP)
    rot = (eighth + far).astype(bf16)
    rot, train_o = lax.optimization_barrier((rot, train_o))
    own = mixed(spread(rot, 8)).reshape(queries, width)
    other = lax.ppermute(own, "core", SWAP)

    partial_inner = call(
        functools.partial(outer_kernel, queries),
        (place, token, own, other, train_rot, train_o, e_out, e_in),
        [SMEM] * 2 + [VMEM] * 6,
        shape((train, half), bf16),
        VMEM,
        2 * queries * width * half + 2 * train * width * half,
        32,
    )
    inner_sum = summed(near(partial_inner.reshape(8, -1, half)))
    inner_sum = jnp.sum(
        lax.all_to_all(spread(inner_sum, 2), "z_a", 0, 0, tiled=True), axis=0
    )
    factor = 1.0 / float(eig_in.shape[0]) ** 0.5
    inner = near(spread((inner_sum * factor).astype(bf16), 8)).reshape(train, half)
    inner_o = lax.ppermute(inner, "core", SWAP)
    partial_out = call(
        back_kernel,
        (core, inner, inner_o, basis_out),
        [SMEM] + [VMEM] * 3,
        shape((train, half), bf16),
        VMEM,
        2 * train * half * width,
        32,
    )
    return summed(lax.all_to_all(partial_out.reshape(16, -1, half), ROW, 0, 0, tiled=True))


def solution(mesh):
    split = Mesh(mesh.devices.reshape(SIZES), ALL)
    placed = (P(None, ROW), P(None, COL), P(None, COL), P(ROW, COL), P(COL, ROW), P(), P())
    return jax.shard_map(
        per_device, mesh=split, in_specs=placed, out_specs=P(ROW, COL), check_vma=False
    )
```

```python
import functools

import jax
import jax.numpy as jnp
import numpy as np
from jax import lax
from jax.experimental import pallas as pl
from jax.experimental.pallas import tpu as pltpu
from jax.sharding import Mesh
from jax.sharding import PartitionSpec as P

ROW = ("z_hi", "y")
CHIPS = ("x", "z_a", "z_b")
COL = (*CHIPS, "core")
ALL = ROW + COL
SIZES = (2, 8, 4, 2, 2, 2)
NEAR = ("x", "z_a")
SWAP = [(0, 1), (1, 0)]
MIB = 1024 * 1024

damping_share = 0.1

bf16 = jnp.bfloat16
f32 = jnp.float32

SMEM = pl.BlockSpec(memory_space=pltpu.SMEM)
VMEM = pl.BlockSpec(memory_space=pltpu.VMEM)
ANY = pl.BlockSpec(memory_space=pl.ANY)


def parity():
    z_hi, y, x, _, z_b = np.indices(SIZES[:-1])
    return (z_hi + y + x + z_b) % 2


def role_ids():
    ids = np.arange(np.prod(SIZES)).reshape(SIZES)
    first = parity()[..., None]
    return np.take_along_axis(ids, np.concatenate([first, 1 - first], axis=-1), axis=-1)


def mixed_groups():
    ids = role_ids()
    along_row = ids[..., 0].transpose(0, 2, 3, 4, 1).reshape(-1, 8).tolist()
    along_col = ids[..., 1].transpose(0, 1, 3, 2, 4).reshape(-1, 8).tolist()
    return along_row + along_col


def mixed_pairs():
    ids = role_ids()
    to = np.empty_like(ids)
    to[..., 0] = ids[::-1, ..., 0]
    to[..., 1] = ids[:, :, :, ::-1, :, 1]
    return list(zip(ids.reshape(-1).tolist(), to.reshape(-1).tolist()))


def role_pairs(source):
    ids = role_ids().reshape(-1, 2)
    return list(zip(ids[:, source].tolist(), ids[:, 1 - source].tolist()))


def dot(a, b):
    return jnp.dot(a, b, preferred_element_type=f32)


def dot_nt(a, b):
    return lax.dot_general(a, b, (((1,), (1,)), ((), ())), preferred_element_type=f32)


def dot_tn(a, b):
    return lax.dot_general(a, b, (((0,), (0,)), ((), ())), preferred_element_type=f32)


def first_kernel(core, token):
    token[0] = core[0]


def rotate_kernel(place, act, grad, b_in, b_out, b_in_o, grad_o, b_out_o, out):
    half = grad.shape[1]

    def joined(low, high):
        out[:, :half] = dot(act[...], low[...]).astype(bf16)
        out[:, half:] = dot(act[...], high[...]).astype(bf16)

    @pl.when((place[3] == 0) & (place[0] == 0))
    def _():
        joined(b_in, b_in_o)

    @pl.when((place[3] == 0) & (place[0] == 1))
    def _():
        joined(b_in_o, b_in)

    @pl.when(place[3] == 1)
    def _():
        out[...] = (dot(grad_o[...], b_out_o[...]) + dot(grad[...], b_out[...])).astype(bf16)


def outer_kernel(queries, place, token, own, other, train, train_o, e_out, e_in, out):
    half = train.shape[1]
    lanes = e_in.shape[1]
    damp = damping_share * (jnp.sum(e_in[...]) / e_in.size) * (jnp.sum(e_out[...]) / e_out.size)
    e_rows = e_in[pl.ds(pl.multiple_of(place[1] * 8, 8), 8), :]
    e_row = jnp.concatenate([e_rows[r : r + 1, :] for r in range(8)], axis=1)
    e_cols = jnp.transpose(e_out[pl.ds(pl.multiple_of(place[2] * 8, 8), 8), :])

    def body(act, grad, first, left, right):
        outer = dot_tn(grad[:, first : first + half], act[...])
        r = first // lanes
        e_col = jnp.concatenate([e_cols[:, r + q : r + q + 1] for q in range(half // lanes)], axis=0)
        scaled = (outer / ((e_col * queries) * e_row + damp * queries)).astype(bf16)
        out[...] = (
            dot_nt(left[...], scaled[:, :half]) + dot_nt(right[...], scaled[:, half:])
        ).astype(bf16)

    for role, (act, grad) in enumerate(((own, other), (other, own))):
        for core, (left, right) in enumerate(((train, train_o), (train_o, train))):

            @pl.when((place[3] == role) & (place[0] == core))
            def _():
                body(act, grad, core * half, left, right)


def back_kernel(core, own, other, b_out, out):
    half = own.shape[1]

    def body(left, right):
        out[...] = (
            dot_nt(left[...], b_out[:, :half]) + dot_nt(right[...], b_out[:, half:])
        ).astype(bf16)

    @pl.when(core[0] == 0)
    def _():
        body(own, other)

    @pl.when(core[0] == 1)
    def _():
        body(other, own)


def call(kernel, args, specs, shapes, out_specs, flops, limit, scratch=()):
    return pl.pallas_call(
        kernel,
        out_shape=shapes,
        in_specs=specs,
        out_specs=out_specs,
        scratch_shapes=scratch,
        compiler_params=pltpu.CompilerParams(vmem_limit_bytes=limit * MIB),
        cost_estimate=pl.CostEstimate(flops=flops, bytes_accessed=4 * MIB, transcendentals=0),
    )(*args)


def summed(pieces):
    return jnp.sum(pieces.astype(f32), axis=0)


def spread(array, n):
    return jnp.broadcast_to(array[None], (n, *array.shape))


def per_device(query_act, query_grad, train_rot, basis_in, basis_out, eig_in, eig_out):
    queries, train = query_act.shape[0], train_rot.shape[0]
    width, half = basis_in.shape
    mixed = functools.partial(
        lax.all_to_all,
        axis_name=ALL,
        split_axis=0,
        concat_axis=0,
        axis_index_groups=mixed_groups(),
        tiled=True,
    )
    near = functools.partial(
        lax.all_to_all, axis_name=NEAR, split_axis=0, concat_axis=0, tiled=True
    )
    shape = jax.ShapeDtypeStruct
    spots = [lax.axis_index(axis) for axis in ("z_hi", "y", "x", "z_b", "core")]
    place = jnp.stack(
        [spots[-1], lax.axis_index(CHIPS), lax.axis_index(ROW), sum(spots) % 2]
    ).astype(jnp.int32)
    core = lax.axis_index("core").astype(jnp.int32).reshape(1)
    e_in, e_out = (e.reshape(-1, 128) for e in (eig_in, eig_out))

    basis_in_o = lax.ppermute(basis_in, ALL, role_pairs(1))
    basis_out_o = lax.ppermute(basis_out, ALL, role_pairs(0))
    grad_o = lax.ppermute(query_grad, ALL, role_pairs(0))

    token = call(
        first_kernel,
        (core,),
        [SMEM],
        shape((1,), jnp.int32),
        SMEM,
        6 * 10**9,
        8,
    )
    basis_in_o, basis_out_o, grad_o, token = lax.optimization_barrier(
        (basis_in_o, basis_out_o, grad_o, token)
    )
    part = call(
        rotate_kernel,
        (place, query_act, query_grad, basis_in, basis_out, basis_in_o, grad_o, basis_out_o),
        [SMEM] + [VMEM] * 7,
        shape((queries, width), bf16),
        VMEM,
        2 * queries * width * width,
        32,
    )
    eighth = summed(mixed(part.reshape(8, -1, width)))
    eighth, train_rot = lax.optimization_barrier((eighth, train_rot))
    far = lax.ppermute(eighth.astype(bf16), ALL, mixed_pairs()).astype(f32)
    train_o = lax.ppermute(train_rot, "core", SWAP)
    rot = (eighth + far).astype(bf16)
    rot, train_o = lax.optimization_barrier((rot, train_o))
    own = mixed(spread(rot, 8)).reshape(queries, width)
    other = lax.ppermute(own, "core", SWAP)

    partial_inner = call(
        functools.partial(outer_kernel, queries),
        (place, token, own, other, train_rot, train_o, e_out, e_in),
        [SMEM] * 2 + [VMEM] * 6,
        shape((train, half), bf16),
        VMEM,
        2 * queries * width * half + 2 * train * width * half,
        32,
    )
    inner_sum = summed(near(partial_inner.reshape(8, -1, half)))
    inner_sum = inner_sum + lax.ppermute(inner_sum, "z_b", SWAP)
    factor = 1.0 / float(eig_in.shape[0]) ** 0.5
    inner = near(spread((inner_sum * factor).astype(bf16), 8)).reshape(train, half)
    inner_o = lax.ppermute(inner, "core", SWAP)
    partial_out = call(
        back_kernel,
        (core, inner, inner_o, basis_out),
        [SMEM] + [VMEM] * 3,
        shape((train, half), bf16),
        VMEM,
        2 * train * half * width,
        32,
    )
    return summed(lax.all_to_all(partial_out.reshape(16, -1, half), ROW, 0, 0, tiled=True))


def solution(mesh):
    split = Mesh(mesh.devices.reshape(SIZES), ALL)
    placed = (P(None, ROW), P(None, COL), P(None, COL), P(ROW, COL), P(COL, ROW), P(), P())
    return jax.shard_map(
        per_device, mesh=split, in_specs=placed, out_specs=P(ROW, COL), check_vma=False
    )
```

```python
import functools

import jax
import jax.numpy as jnp
import numpy as np
from jax import lax
from jax.experimental import pallas as pl
from jax.experimental.pallas import tpu as pltpu
from jax.sharding import Mesh
from jax.sharding import PartitionSpec as P

ROW = ("z_hi", "y")
CHIPS = ("x", "z_a", "z_b")
COL = (*CHIPS, "core")
ALL = ROW + COL
SIZES = (2, 8, 4, 2, 2, 2)
NEAR = ("x", "z_b")
SWAP = [(0, 1), (1, 0)]
MIB = 1024 * 1024

damping_share = 0.1

bf16 = jnp.bfloat16
f32 = jnp.float32

SMEM = pl.BlockSpec(memory_space=pltpu.SMEM)
VMEM = pl.BlockSpec(memory_space=pltpu.VMEM)
ANY = pl.BlockSpec(memory_space=pl.ANY)


def parity():
    z_hi, y, x, _, z_b = np.indices(SIZES[:-1])
    return (z_hi + y + x + z_b) % 2


def role_ids():
    ids = np.arange(np.prod(SIZES)).reshape(SIZES)
    first = parity()[..., None]
    return np.take_along_axis(ids, np.concatenate([first, 1 - first], axis=-1), axis=-1)


def mixed_groups():
    ids = role_ids()
    along_row = ids[..., 0].transpose(0, 2, 3, 4, 1).reshape(-1, 8).tolist()
    along_col = ids[..., 1].transpose(0, 1, 3, 2, 4).reshape(-1, 8).tolist()
    return along_row + along_col


def mixed_pairs():
    ids = role_ids()
    to = np.empty_like(ids)
    to[..., 0] = ids[::-1, ..., 0]
    to[..., 1] = ids[:, :, :, ::-1, :, 1]
    return list(zip(ids.reshape(-1).tolist(), to.reshape(-1).tolist()))


def role_pairs(source):
    ids = role_ids().reshape(-1, 2)
    return list(zip(ids[:, source].tolist(), ids[:, 1 - source].tolist()))


def dot(a, b):
    return jnp.dot(a, b, preferred_element_type=f32)


def dot_nt(a, b):
    return lax.dot_general(a, b, (((1,), (1,)), ((), ())), preferred_element_type=f32)


def dot_tn(a, b):
    return lax.dot_general(a, b, (((0,), (0,)), ((), ())), preferred_element_type=f32)


def first_kernel(core, token):
    token[0] = core[0]


def rotate_kernel(place, act, grad, b_in, b_out, b_in_o, grad_o, b_out_o, out):
    half = grad.shape[1]

    def joined(low, high):
        out[:, :half] = dot(act[...], low[...]).astype(bf16)
        out[:, half:] = dot(act[...], high[...]).astype(bf16)

    @pl.when((place[3] == 0) & (place[0] == 0))
    def _():
        joined(b_in, b_in_o)

    @pl.when((place[3] == 0) & (place[0] == 1))
    def _():
        joined(b_in_o, b_in)

    @pl.when(place[3] == 1)
    def _():
        out[...] = (dot(grad_o[...], b_out_o[...]) + dot(grad[...], b_out[...])).astype(bf16)


def outer_kernel(queries, place, token, own, other, train, train_o, e_out, e_in, out):
    half = train.shape[1]
    lanes = e_in.shape[1]
    damp = damping_share * (jnp.sum(e_in[...]) / e_in.size) * (jnp.sum(e_out[...]) / e_out.size)
    e_rows = e_in[pl.ds(pl.multiple_of(place[1] * 8, 8), 8), :]
    e_row = jnp.concatenate([e_rows[r : r + 1, :] for r in range(8)], axis=1)
    e_cols = jnp.transpose(e_out[pl.ds(pl.multiple_of(place[2] * 8, 8), 8), :])

    def body(act, grad, first, left, right):
        outer = dot_tn(grad[:, first : first + half], act[...])
        r = first // lanes
        e_col = jnp.concatenate([e_cols[:, r + q : r + q + 1] for q in range(half // lanes)], axis=0)
        scaled = (outer / ((e_col * queries) * e_row + damp * queries)).astype(bf16)
        out[...] = (
            dot_nt(left[...], scaled[:, :half]) + dot_nt(right[...], scaled[:, half:])
        ).astype(bf16)

    for role, (act, grad) in enumerate(((own, other), (other, own))):
        for core, (left, right) in enumerate(((train, train_o), (train_o, train))):

            @pl.when((place[3] == role) & (place[0] == core))
            def _():
                body(act, grad, core * half, left, right)


def back_kernel(core, own, other, b_out, out):
    half = own.shape[1]

    def body(left, right):
        out[...] = (
            dot_nt(left[...], b_out[:, :half]) + dot_nt(right[...], b_out[:, half:])
        ).astype(bf16)

    @pl.when(core[0] == 0)
    def _():
        body(own, other)

    @pl.when(core[0] == 1)
    def _():
        body(other, own)


def call(kernel, args, specs, shapes, out_specs, flops, limit, scratch=()):
    return pl.pallas_call(
        kernel,
        out_shape=shapes,
        in_specs=specs,
        out_specs=out_specs,
        scratch_shapes=scratch,
        compiler_params=pltpu.CompilerParams(vmem_limit_bytes=limit * MIB),
        cost_estimate=pl.CostEstimate(flops=flops, bytes_accessed=4 * MIB, transcendentals=0),
    )(*args)


def summed(pieces):
    return jnp.sum(pieces.astype(f32), axis=0)


def spread(array, n):
    return jnp.broadcast_to(array[None], (n, *array.shape))


def per_device(query_act, query_grad, train_rot, basis_in, basis_out, eig_in, eig_out):
    queries, train = query_act.shape[0], train_rot.shape[0]
    width, half = basis_in.shape
    mixed = functools.partial(
        lax.all_to_all,
        axis_name=ALL,
        split_axis=0,
        concat_axis=0,
        axis_index_groups=mixed_groups(),
        tiled=True,
    )
    near = functools.partial(
        lax.all_to_all, axis_name=NEAR, split_axis=0, concat_axis=0, tiled=True
    )
    shape = jax.ShapeDtypeStruct
    spots = [lax.axis_index(axis) for axis in ("z_hi", "y", "x", "z_b", "core")]
    place = jnp.stack(
        [spots[-1], lax.axis_index(CHIPS), lax.axis_index(ROW), sum(spots) % 2]
    ).astype(jnp.int32)
    core = lax.axis_index("core").astype(jnp.int32).reshape(1)
    e_in, e_out = (e.reshape(-1, 128) for e in (eig_in, eig_out))

    basis_in_o = lax.ppermute(basis_in, ALL, role_pairs(1))
    basis_out_o = lax.ppermute(basis_out, ALL, role_pairs(0))
    grad_o = lax.ppermute(query_grad, ALL, role_pairs(0))

    token = call(
        first_kernel,
        (core,),
        [SMEM],
        shape((1,), jnp.int32),
        SMEM,
        6 * 10**9,
        8,
    )
    basis_in_o, basis_out_o, grad_o, token = lax.optimization_barrier(
        (basis_in_o, basis_out_o, grad_o, token)
    )
    part = call(
        rotate_kernel,
        (place, query_act, query_grad, basis_in, basis_out, basis_in_o, grad_o, basis_out_o),
        [SMEM] + [VMEM] * 7,
        shape((queries, width), bf16),
        VMEM,
        2 * queries * width * width,
        32,
    )
    eighth = summed(mixed(part.reshape(8, -1, width)))
    eighth, train_rot = lax.optimization_barrier((eighth, train_rot))
    far = lax.ppermute(eighth.astype(bf16), ALL, mixed_pairs()).astype(f32)
    train_o = lax.ppermute(train_rot, "core", SWAP)
    rot = (eighth + far).astype(bf16)
    rot, train_o = lax.optimization_barrier((rot, train_o))
    own = mixed(spread(rot, 8)).reshape(queries, width)
    other = lax.ppermute(own, "core", SWAP)

    partial_inner = call(
        functools.partial(outer_kernel, queries),
        (place, token, own, other, train_rot, train_o, e_out, e_in),
        [SMEM] * 2 + [VMEM] * 6,
        shape((train, half), bf16),
        VMEM,
        2 * queries * width * half + 2 * train * width * half,
        32,
    )
    inner_sum = summed(near(partial_inner.reshape(8, -1, half)))
    far_inner = lax.ppermute(inner_sum.astype(bf16), "z_a", SWAP)
    inner_sum = inner_sum + far_inner.astype(f32)
    factor = 1.0 / float(eig_in.shape[0]) ** 0.5
    inner = near(spread((inner_sum * factor).astype(bf16), 8)).reshape(train, half)
    inner_o = lax.ppermute(inner, "core", SWAP)
    partial_out = call(
        back_kernel,
        (core, inner, inner_o, basis_out),
        [SMEM] + [VMEM] * 3,
        shape((train, half), bf16),
        VMEM,
        2 * train * half * width,
        32,
    )
    return summed(lax.all_to_all(partial_out.reshape(16, -1, half), ROW, 0, 0, tiled=True))


def solution(mesh):
    split = Mesh(mesh.devices.reshape(SIZES), ALL)
    placed = (P(None, ROW), P(None, COL), P(None, COL), P(ROW, COL), P(COL, ROW), P(), P())
    return jax.shard_map(
        per_device, mesh=split, in_specs=placed, out_specs=P(ROW, COL), check_vma=False
    )
```
